32 devices in a mesh: grp: 2 (over y), leaf: 4 (over z), vec: 2 (over x), sub: 2 (over core).
Axes of the slice: x: 2, y: 2, z: 4, core: 2. Of those that a mesh axis runs over, the one named last changes fastest.
Arguments:
- vectors: bfloat16 [128, 32768], P(('grp', 'vec'), ('leaf', 'sub')), parts along dimension 0, may hold values from -6 to 6
- coords: bfloat16 [6, 32768], P('grp', ('leaf', 'sub')), parts along dimension 0, may hold values from 0 to 1
- point_order: int32 [65536], P(('grp', 'leaf', 'sub')), parts along dimension 0, may hold values from 0 to 32767, as said below
- leaf_basis: bfloat16 [256, 64, 256], P(('grp', 'leaf', 'sub')), parts along dimension 0, may hold values from -0.375 to 0.375
- transfer_local: bfloat16 [480, 4096], P(('grp', 'leaf', 'sub')), parts along dimension 0, may hold values from -0.5 to 0.5
- transfer_top: bfloat16 [24, 4096], P('grp'), parts along dimension 0, may hold values from -0.5 to 0.5
- partners_local: int32 [496, 4], P(('grp', 'leaf', 'sub')), parts along dimension 0, may hold values from 0 to 247, as said below
- coupling_local: bfloat16 [496, 4, 4096], P(('grp', 'leaf', 'sub')), parts along dimension 0, may hold values from -1 to 1
- top_partners: int32 [12, 2], P('grp'), parts along dimension 0, may hold values from 0 to 3, as said below
- top_coupling: bfloat16 [12, 2, 4096], P('grp'), parts along dimension 0, may hold values from -2.828427 to 2.828427
Outputs:
- product: bfloat16 [128, 32768], P(('grp', 'vec'), ('leaf', 'sub')), parts along dimension 0
The draws below stay inside these ranges and needn't reach their ends.
There are 2 independent parts, one for each index of `grp`. The reference program is written for one: setup_inputs(seed, part) draws one part's arguments, and reference() takes and returns one part's arrays. A program takes and returns all parts, laid end to end along the dimension named above; each array names one. Nothing has to cross between parts.
Inputs may be any that keep to these rules, and one draw needn't show every extreme that they name: `point_order`: A permutation of the positions. Of the 4096 points in one aligned block of the input order, at most 1408 go to one subtree's block of positions, and one subtree receives exactly 1408 from one block in every draw. `partners_local`: each entry is a row number as in the steps of a node on the same level as the row's own node, in the same subtree or in the one just before or after it, never the node itself. `top_partners`: each entry is another node of the same top level.
All inputs are finite; a program needn't handle non-finite values.
Results may differ from the reference program's by a relative error of at most 0.011.
Values may be sent and summed in bfloat16 or wider, within the bound.
A program may use at most 64 MiB of HBM per device.

```python
import jax
import jax.numpy as jnp
import numpy as np
from jax import lax

LEAF_PTS = 256
RANK = 64
NVEC = 64
LEAVES_DEV = 16
PARTNERS = 4
TOP_PARTNERS = 2
SUBTREES = 8
DEV_PTS = 4096
POINTS = 32768
LOCAL_NODES = 31
EVEN_SHARE = 512
EXTRA_SHARE = 128


BOX_SIDE = 0.0625


def cluster_positions(key):
    key = jax.random.fold_in(key, 11)
    key_one, key_two, key_three = jax.random.split(key, 3)
    drawn = EVEN_SHARE - EXTRA_SHARE
    heavy = SUBTREES * EXTRA_SHARE
    sigma = jax.random.permutation(key_one, SUBTREES)
    device_ids = jnp.arange(SUBTREES, dtype=jnp.int32)
    counts = drawn + heavy * (sigma[:, None] == device_ids[None, :]).astype(jnp.int32)
    row_end = jnp.cumsum(counts, axis=1)
    row_start = row_end - counts
    column_start = jnp.cumsum(counts, axis=0) - counts
    slots = jnp.arange(DEV_PTS, dtype=jnp.int32)
    target_dev = jnp.sum((row_end[:, None, :] <= slots[None, :, None]).astype(jnp.int32), axis=2)
    within = slots[None, :] - jnp.take_along_axis(row_start, target_dev, axis=1)
    arrival = jnp.take_along_axis(column_start, target_dev, axis=1) + within
    dest_keys = jax.random.split(key_two, SUBTREES)
    dest_perm = jax.vmap(lambda one_key: jax.random.permutation(one_key, DEV_PTS))(dest_keys).astype(jnp.int32)
    flat_perm = dest_perm.reshape(SUBTREES * DEV_PTS)
    position = target_dev * DEV_PTS + flat_perm[target_dev * DEV_PTS + arrival]
    source_keys = jax.random.split(key_three, SUBTREES)
    shuffle = jax.vmap(lambda one_key: jax.random.permutation(one_key, DEV_PTS))(source_keys).astype(jnp.int32)
    source_ids = jnp.broadcast_to(device_ids[:, None], (SUBTREES, DEV_PTS))
    result = jnp.zeros((SUBTREES, DEV_PTS), jnp.int32).at[source_ids, shuffle].set(position)
    return result.reshape(SUBTREES * DEV_PTS).astype(jnp.int32)


def draw_point_order(key, part):
    return cluster_positions(key)


def draw_coords(key, part):
    positions = cluster_positions(key)
    key = jax.random.fold_in(key, 61)
    leaf_total = SUBTREES * LEAVES_DEV
    width_boxes = min(leaf_total, 16)
    depth_boxes = min(leaf_total // width_boxes, 16)
    leaf_index = positions // LEAF_PTS
    row_index = leaf_index // width_boxes
    along_row = leaf_index % width_boxes
    layer_index = row_index // depth_boxes
    along_layer = row_index % depth_boxes
    box_first = jnp.where(row_index % 2 == 0, along_row, width_boxes - 1 - along_row)
    box_second = jnp.where(layer_index % 2 == 0, along_layer, depth_boxes - 1 - along_layer)
    corner = jnp.stack([box_first, box_second, layer_index], axis=0).astype(jnp.float32) * BOX_SIDE
    jitter = jax.random.uniform(key, (3, POINTS), jnp.float32)
    return (corner + jitter * BOX_SIDE).astype(jnp.bfloat16)


def level_tables():
    levels = LEAVES_DEV.bit_length()
    level_of = np.concatenate([np.full(LEAVES_DEV >> step, step) for step in range(levels)])
    offset_of = np.concatenate([np.full(LEAVES_DEV >> step, 2 * LEAVES_DEV - 2 * (LEAVES_DEV >> step)) for step in range(levels)])
    index_of = np.concatenate([np.arange(LEAVES_DEV >> step) for step in range(levels)])
    count_of = np.concatenate([np.full(LEAVES_DEV >> step, LEAVES_DEV >> step) for step in range(levels)])
    return (level_of, offset_of, index_of, count_of)


def draw_partners_local(key, part):
    key = jax.random.fold_in(key, 21)
    key_one, key_two = jax.random.split(key)
    level_of, offset_of, index_of, count_of = level_tables()
    device_ids = jnp.arange(SUBTREES, dtype=jnp.int32)[:, None, None]
    shape = (SUBTREES, LOCAL_NODES, PARTNERS)
    source = device_ids + jax.random.randint(key_one, shape, -1, 2)
    source = jnp.where(source < 0, 1, source)
    source = jnp.where(source >= SUBTREES, SUBTREES - 2, source)
    pick = jax.random.randint(key_two, shape, 0, 1 << 30) % jnp.asarray(count_of, jnp.int32)[None, :, None]
    itself = (source == device_ids) & (pick == jnp.asarray(index_of, jnp.int32)[None, :, None])
    beside = jnp.where(device_ids + 1 < SUBTREES, device_ids + 1, device_ids - 1)
    source = jnp.where(itself, beside, source)
    number = source * LOCAL_NODES + jnp.asarray(offset_of, jnp.int32)[None, :, None] + pick
    return number.reshape(SUBTREES * LOCAL_NODES, PARTNERS).astype(jnp.int32)


def draw_coupling_local(key, part):
    key = jax.random.fold_in(key, 31)
    level_of, offset_of, index_of, count_of = level_tables()
    scale_row = np.tile(2.0 ** (level_of / 2.0) / np.sqrt(PARTNERS * RANK), SUBTREES).astype(np.float32)
    shape = (SUBTREES * LOCAL_NODES, PARTNERS, RANK * RANK)
    values = jax.random.truncated_normal(key, -4.0, 4.0, shape, jnp.float32)
    return (values * jnp.asarray(scale_row)[:, None, None]).astype(jnp.bfloat16)


def draw_top_partners(key, part):
    key = jax.random.fold_in(key, 41)
    half_top = SUBTREES // 2
    quarter_top = SUBTREES // 4
    count_of = np.concatenate([np.full(half_top, half_top), np.full(quarter_top, quarter_top)]).astype(np.int32)
    row_of = np.concatenate([np.arange(half_top), np.arange(quarter_top)]).astype(np.int32)
    raw_hop = jax.random.randint(key, (half_top + quarter_top, TOP_PARTNERS), 0, 1 << 30)
    hop_size = raw_hop % jnp.asarray(count_of - 1)[:, None] + 1
    return ((jnp.asarray(row_of)[:, None] + hop_size) % jnp.asarray(count_of)[:, None]).astype(jnp.int32)


def draw_top_coupling(key, part):
    key = jax.random.fold_in(key, 51)
    half_top = SUBTREES // 2
    quarter_top = SUBTREES // 4
    lowest = LEAVES_DEV.bit_length() - 1
    level_of = np.concatenate([np.full(half_top, lowest + 1), np.full(quarter_top, lowest + 2)])
    scale_row = (2.0 ** (level_of / 2.0) / np.sqrt(TOP_PARTNERS * RANK)).astype(np.float32)
    shape = (half_top + quarter_top, TOP_PARTNERS, RANK * RANK)
    values = jax.random.truncated_normal(key, -4.0, 4.0, shape, jnp.float32)
    return (values * jnp.asarray(scale_row)[:, None, None]).astype(jnp.bfloat16)


def block_levels(rng, extent, cuts, low, top_value):
    loudness = 1.0
    for dim, shards_of in cuts:
        steps = jax.random.uniform(jax.random.fold_in(jax.random.fold_in(rng, 6), dim), (shards_of,), jnp.float32, low / len(cuts), top_value / len(cuts))
        loudness = loudness * jnp.repeat(jnp.exp(steps), extent[dim] // shards_of).reshape((-1,) + (1,) * (len(extent) - 1 - dim))
    return loudness


def normal_values(own_key, shape, deviation, most, cuts=(), held_as=jnp.bfloat16):
    values = jax.random.normal(own_key, shape, jnp.float32) * deviation
    if len(cuts) > 0:
        values = block_levels(own_key, shape, cuts, -0.22, 0.18) * values
    return jnp.clip(values, min=-most, max=most).astype(held_as)


def setup_inputs(seed: int = 0, part: int = 0) -> dict:
    keys = jax.random.split(jax.random.key(seed), 11)
    part_splits = jax.random.split(jax.random.fold_in(keys[10], part), 11)
    return {
        "vectors": normal_values(part_splits[0], (NVEC, POINTS), 1.0, 6.0, ((0, 2), (1, 8))),
        "coords": draw_coords(jax.random.fold_in(jax.random.fold_in(keys[10], part), 71), part),
        "point_order": draw_point_order(jax.random.fold_in(jax.random.fold_in(keys[10], part), 71), part),
        "leaf_basis": normal_values(part_splits[3], (SUBTREES * LEAVES_DEV, RANK, LEAF_PTS), LEAF_PTS ** -0.5, 0.375, ((0, 8),)),
        "transfer_local": normal_values(part_splits[4], (SUBTREES * (2 * LEAVES_DEV - 2), RANK * RANK), (2 * RANK) ** -0.5, 0.5, ((0, 8),)),
        "transfer_top": normal_values(part_splits[5], (SUBTREES + SUBTREES // 2, RANK * RANK), (2 * RANK) ** -0.5, 0.5),
        "partners_local": draw_partners_local(jax.random.fold_in(jax.random.fold_in(keys[10], part), 71), part),
        "coupling_local": draw_coupling_local(jax.random.fold_in(jax.random.fold_in(keys[10], part), 71), part),
        "top_partners": draw_top_partners(jax.random.fold_in(jax.random.fold_in(keys[10], part), 71), part),
        "top_coupling": draw_top_coupling(jax.random.fold_in(jax.random.fold_in(keys[10], part), 71), part),
    }


ROOT_THREE = 1.7320508075688772
LENGTH_SCALE = 0.0125
KERNEL_GAIN = 0.25

def rounded(values):
    return lax.optimization_barrier(values.astype(jnp.bfloat16)).astype(jnp.float32)

def matern(target, source, amplitude):
    delta_x = target[0][:, :, None] - source[0][:, None, :]
    delta_y = target[1][:, :, None] - source[1][:, None, :]
    delta_z = target[2][:, :, None] - source[2][:, None, :]
    scaled = ROOT_THREE / LENGTH_SCALE * jnp.sqrt(delta_x * delta_x + delta_y * delta_y + delta_z * delta_z)
    return ((1.0 + scaled) * jnp.exp(-scaled) * amplitude).astype(jnp.bfloat16)

def near_field(padded, leaf_count, amplitude):
    row_total = padded.shape[0]
    vec_rows = row_total - 3
    leaf_pts = padded.shape[1] // (leaf_count + 2)
    blocks = padded.reshape(row_total, leaf_count + 2, leaf_pts)
    window = jnp.concatenate([blocks[:, :leaf_count], blocks[:, 1:leaf_count + 1], blocks[:, 2:]], axis=2)
    middle = blocks[:, 1:leaf_count + 1, :]
    group_size = min(leaf_count, 8)

    def one_group(begin_at):
        window_part = lax.dynamic_slice_in_dim(window, begin_at, group_size, 1)
        middle_part = lax.dynamic_slice_in_dim(middle, begin_at, group_size, 1)
        kernel = matern(middle_part[vec_rows:].astype(jnp.float32), window_part[vec_rows:].astype(jnp.float32), amplitude)
        return jnp.einsum('glm,vgm->vgl', kernel.astype(jnp.float32), window_part[:vec_rows].astype(jnp.float32))
    starts = jnp.arange(leaf_count // group_size, dtype=jnp.int32) * group_size
    pieces = lax.map(one_group, starts)
    return jnp.transpose(pieces, (1, 0, 2, 3)).reshape(vec_rows, leaf_count * leaf_pts)

def reference(vectors, coords, point_order, leaf_basis, transfer_local, transfer_top, partners_local, coupling_local, top_partners, top_coupling):
    subtrees = SUBTREES
    leaves = LEAVES_DEV
    node_count = LOCAL_NODES
    rank_dim = RANK
    vec_rows = NVEC
    levels = leaves.bit_length()
    amplitude = KERNEL_GAIN
    packed = jnp.concatenate([vectors, coords], axis=0)
    arranged = jnp.zeros_like(packed).at[:, point_order].set(packed)
    zero_rim = jnp.zeros((vec_rows + 3, LEAF_PTS), packed.dtype)
    padded = jnp.concatenate([zero_rim, arranged, zero_rim], axis=1)
    near_part = near_field(padded, subtrees * leaves, amplitude)
    leaf_rows = arranged[:vec_rows].reshape(vec_rows, subtrees * leaves, LEAF_PTS).astype(jnp.float32)
    coefficients = jnp.einsum('vtl,tal->tva', leaf_rows, leaf_basis.astype(jnp.float32)).astype(jnp.bfloat16)
    per_level = [coefficients.reshape(subtrees, leaves, vec_rows, rank_dim)]
    transfers = transfer_local.astype(jnp.float32).reshape(subtrees, 2 * leaves - 2, rank_dim, rank_dim)
    offset = 0
    level_count = leaves
    for level_idx in range(levels - 1):
        pair_mats = transfers[:, offset:offset + level_count].reshape(subtrees, level_count // 2, 2, rank_dim, rank_dim)
        pair_coef = per_level[-1].astype(jnp.float32).reshape(subtrees, level_count // 2, 2, vec_rows, rank_dim)
        per_level.append(jnp.einsum('dicab,dicvb->diva', pair_mats, pair_coef).astype(jnp.bfloat16))
        offset = offset + level_count
        level_count = level_count // 2
    all_levels = jnp.concatenate(per_level, axis=1).reshape(subtrees * node_count, vec_rows, rank_dim)
    sources = all_levels[partners_local].astype(jnp.float32)
    couplings = coupling_local.astype(jnp.float32).reshape(subtrees * node_count, PARTNERS, rank_dim, rank_dim)
    local_out = jnp.einsum('gkab,gkvb->gva', couplings, sources).reshape(subtrees, node_count, vec_rows, rank_dim)
    half_top = subtrees // 2
    quarter_top = subtrees // 4
    top_mats = transfer_top.astype(jnp.float32).reshape(subtrees + half_top, rank_dim, rank_dim)
    roots = per_level[-1].astype(jnp.float32).reshape(half_top, 2, vec_rows, rank_dim)
    level_one = jnp.einsum('icab,icvb->iva', top_mats[:subtrees].reshape(half_top, 2, rank_dim, rank_dim), roots).astype(jnp.bfloat16)
    level_two = jnp.einsum('icab,icvb->iva', top_mats[subtrees:].reshape(quarter_top, 2, rank_dim, rank_dim), level_one.astype(jnp.float32).reshape(quarter_top, 2, vec_rows, rank_dim)).astype(jnp.bfloat16)
    top_coef = jnp.concatenate([level_one, level_two], axis=0)
    level_shift = jnp.where(jnp.arange(half_top + quarter_top, dtype=jnp.int32)[:, None] >= half_top, half_top, 0).astype(jnp.int32)
    top_sources = top_coef[top_partners + level_shift].astype(jnp.float32)
    top_out = jnp.einsum('gkab,gkvb->gva', top_coupling.astype(jnp.float32).reshape(half_top + quarter_top, TOP_PARTNERS, rank_dim, rank_dim), top_sources)
    middle_top = top_out[:half_top] + jnp.einsum('icab,iva->icvb', top_mats[subtrees:].reshape(quarter_top, 2, rank_dim, rank_dim), rounded(top_out[half_top:])).reshape(half_top, vec_rows, rank_dim)
    root_down = jnp.einsum('icab,iva->icvb', top_mats[:subtrees].reshape(half_top, 2, rank_dim, rank_dim), rounded(middle_top)).reshape(subtrees, vec_rows, rank_dim)
    current = (local_out[:, node_count - 1] + root_down)[:, None]
    offset = node_count - 1
    level_count = 1
    for level_idx in range(levels - 1):
        child_count = level_count * 2
        offset = offset - child_count
        pair_mats = transfers[:, offset:offset + child_count].reshape(subtrees, level_count, 2, rank_dim, rank_dim)
        downward = jnp.einsum('dicab,diva->dicvb', pair_mats, rounded(current)).reshape(subtrees, child_count, vec_rows, rank_dim)
        current = local_out[:, offset:offset + child_count] + downward
        level_count = child_count
    leaf_coef = rounded(current).reshape(subtrees * leaves, vec_rows, rank_dim)
    far_field = jnp.einsum('tva,tal->vtl', leaf_coef, leaf_basis.astype(jnp.float32)).reshape(vec_rows, POINTS)
    answer = (far_field + near_part).astype(jnp.bfloat16)
    return answer[:, point_order]
```

```python
import functools

import jax
import jax.numpy as jnp
from jax import lax
from jax.experimental import pallas as pl
from jax.experimental.pallas import tpu as pltpu
from jax.sharding import PartitionSpec as P

ROOT_THREE = 1.7320508075688772
LENGTH_SCALE = 0.0125
KERNEL_GAIN = 0.25
LOG2_E = 1.4426950408889634
MESH = pl.DeviceIdType.MESH
VMEM_LIMIT = 56 * 1024 * 1024
CHUNK = 1024
FIELDS = 8


def for_each_block(lines, pairs, sems, process):
    send_sem, pass_sem, recv_sem = sems
    mine = lax.axis_index("leaf")
    core = lax.axis_index("sub")
    other = 1 - core
    me = mine * 2 + core
    barrier = pltpu.get_barrier_semaphore()
    for hop in range(1, lines):
        target = lax.rem(mine + hop, lines)
        pl.semaphore_signal(barrier, inc=1, device_id={"leaf": target}, device_id_type=MESH)
    pl.semaphore_signal(barrier, inc=1, device_id={"sub": other}, device_id_type=MESH)
    pl.semaphore_wait(barrier, lines)

    def sends(hop):
        target = lax.rem(mine + hop, lines)
        return [
            pltpu.make_async_remote_copy(
                src_ref=own,
                dst_ref=held.at[me],
                send_sem=send_sem.at[which, hop],
                recv_sem=recv_sem.at[which, me],
                device_id={"leaf": target},
                device_id_type=MESH,
            )
            for which, (own, held) in enumerate(pairs)
        ]

    def across(hop, block):
        return [
            pltpu.make_async_remote_copy(
                src_ref=held.at[block],
                dst_ref=held.at[block],
                send_sem=pass_sem.at[which, hop],
                recv_sem=recv_sem.at[which, block],
                device_id={"sub": other},
                device_id_type=MESH,
            )
            for which, (own, held) in enumerate(pairs)
        ]

    def begin(hop, carry):
        for copy in sends(hop):
            copy.start()
        return carry

    lax.fori_loop(1, lines, begin, 0)
    for own, held in pairs:
        held[me] = own[...]

    def step(hop, carry):
        line = lax.rem(mine + lines - hop, lines)
        near_block = line * 2 + core
        far_block = line * 2 + other

        @pl.when(hop > 0)
        def _():
            for copy in across(hop, near_block):
                copy.wait_recv()

        for copy in across(hop, near_block):
            copy.start()
        process(near_block)
        for copy in across(hop, far_block):
            copy.wait_recv()
        process(far_block)
        return carry

    lax.fori_loop(0, lines, step, 0)

    def finish(hop, carry):
        for copy in sends(hop):
            copy.wait_send()
        return carry

    lax.fori_loop(1, lines, finish, 0)

    def finish_across(hop, carry):
        for copy in across(hop, lax.rem(mine + lines - hop, lines) * 2 + core):
            copy.wait_send()
        return carry

    lax.fori_loop(0, lines, finish_across, 0)


def arrange_kernel(
    lines, leaves, x_ref, aux_ref, v_out, c_out, x_all, aux_all, total, send_sem, pass_sem, recv_sem
):
    me = lax.axis_index("leaf") * 2 + lax.axis_index("sub")
    rows = x_ref.shape[0]
    dev_pts = x_ref.shape[1]
    leaf_pts = v_out.shape[1]
    slots = leaves + 2
    slot_pad = -(-slots // 8) * 8
    total[...] = jnp.zeros_like(total)

    def process(block):
        aux = aux_all[block].astype(jnp.float32)
        for part in range(dev_pts // CHUNK):
            fields = aux[part * FIELDS : (part + 1) * FIELDS]
            x = x_all[block, :, part * CHUNK : (part + 1) * CHUNK]
            slot = (fields[5:6] - me.astype(jnp.float32)) * leaves + fields[4:5] + 1.0
            slot_here = jnp.broadcast_to(slot, (rows, CHUNK)).astype(jnp.int32)
            zero = jnp.zeros_like(x)
            parts = [jnp.where(slot_here == k, x, zero) for k in range(slots)]
            slot_ids = lax.broadcasted_iota(jnp.int32, (slot_pad, CHUNK), 0)
            chosen = slot_ids == jnp.broadcast_to(slot, (slot_pad, CHUNK)).astype(jnp.int32)
            for axis in range(3):
                row = jnp.broadcast_to(fields[axis : axis + 1], (slot_pad, CHUNK))
                parts.append(jnp.where(chosen, row, 0.0).astype(jnp.bfloat16))
            place_ids = lax.broadcasted_iota(jnp.int32, (leaf_pts, CHUNK), 0)
            place = jnp.broadcast_to(fields[3:4].astype(jnp.int32), (leaf_pts, CHUNK))
            one_hot = jnp.where(place_ids == place, 1.0, 0.0).astype(jnp.bfloat16)
            total[...] += lax.dot_general(
                jnp.concatenate(parts, axis=0),
                one_hot,
                (((1,), (1,)), ((), ())),
                preferred_element_type=jnp.float32,
            )

    pairs = ((x_ref, x_all), (aux_ref, aux_all))
    for_each_block(lines, pairs, (send_sem, pass_sem, recv_sem), process)
    v_out[...] = total[: slots * rows, :].astype(jnp.bfloat16)
    c_out[...] = jnp.zeros_like(c_out)
    for slot in range(slots):
        for axis in range(3):
            at = slots * rows + axis * slot_pad + slot
            c_out[slot * 8 + axis : slot * 8 + axis + 1, :] = total[at : at + 1, :]


def arrange(lines, leaves, leaf_pts, x, aux):
    rows, dev_pts = x.shape
    devices = lines * 2
    slots = leaves + 2
    slot_pad = -(-slots // 8) * 8
    return pl.pallas_call(
        functools.partial(arrange_kernel, lines, leaves),
        out_shape=(
            jax.ShapeDtypeStruct((slots * rows, leaf_pts), jnp.bfloat16),
            jax.ShapeDtypeStruct((slots * 8, leaf_pts), jnp.float32),
        ),
        in_specs=[pl.BlockSpec(memory_space=pltpu.VMEM)] * 2,
        out_specs=(pl.BlockSpec(memory_space=pltpu.VMEM),) * 2,
        scratch_shapes=[
            pltpu.VMEM((devices,) + x.shape, jnp.bfloat16),
            pltpu.VMEM((devices,) + aux.shape, jnp.bfloat16),
            pltpu.VMEM((slots * rows + 3 * slot_pad, leaf_pts), jnp.float32),
            pltpu.SemaphoreType.DMA((2, lines)),
            pltpu.SemaphoreType.DMA((2, lines)),
            pltpu.SemaphoreType.DMA((2, devices)),
        ],
        compiler_params=pltpu.CompilerParams(
            collective_id=0, has_side_effects=True, vmem_limit_bytes=VMEM_LIMIT
        ),
        name="arrange",
    )(x, aux)


def hand_back_kernel(
    lines, leaves, y_ref, order_ref, out_ref, y_all, one_hot, leaf_at, send_sem, pass_sem, recv_sem
):
    leaf_pts = y_ref.shape[1]
    rows = y_ref.shape[0] // leaves
    dev_pts = order_ref.shape[1]
    order = order_ref[...]
    leaf_at[...] = order // leaf_pts
    for part in range(dev_pts // CHUNK):
        at = slice(part * CHUNK, (part + 1) * CHUNK)
        place_ids = lax.broadcasted_iota(jnp.int32, (leaf_pts, CHUNK), 0)
        place = jnp.broadcast_to(order[:, at] % leaf_pts, (leaf_pts, CHUNK))
        one_hot[:, at] = jnp.where(place_ids == place, 1.0, 0.0).astype(jnp.bfloat16)
    out_ref[...] = jnp.zeros_like(out_ref)

    def process(block):
        y = y_all[block]

        def chunk(part, carry):
            at = pl.ds(pl.multiple_of(part * CHUNK, CHUNK), CHUNK)
            found = jnp.dot(y, one_hot[:, at], preferred_element_type=jnp.float32)
            leaf = jnp.broadcast_to(leaf_at[:, at] - block * leaves, (rows, CHUNK))
            got = jnp.zeros((rows, CHUNK), jnp.float32)
            for k in range(leaves):
                got = jnp.where(leaf == k, found[k * rows : (k + 1) * rows], got)
            out_ref[:, at] += got.astype(jnp.bfloat16)
            return carry

        lax.fori_loop(0, dev_pts // CHUNK, chunk, 0)

    for_each_block(lines, ((y_ref, y_all),), (send_sem, pass_sem, recv_sem), process)


def hand_back(lines, leaves, y, order):
    devices = lines * 2
    rows = y.shape[0] // leaves
    dev_pts = order.shape[1]
    return pl.pallas_call(
        functools.partial(hand_back_kernel, lines, leaves),
        out_shape=jax.ShapeDtypeStruct((rows, dev_pts), jnp.bfloat16),
        in_specs=[pl.BlockSpec(memory_space=pltpu.VMEM)] * 2,
        out_specs=pl.BlockSpec(memory_space=pltpu.VMEM),
        scratch_shapes=[
            pltpu.VMEM((devices,) + y.shape, jnp.bfloat16),
            pltpu.VMEM((y.shape[1], dev_pts), jnp.bfloat16),
            pltpu.VMEM((1, dev_pts), jnp.int32),
            pltpu.SemaphoreType.DMA((1, lines)),
            pltpu.SemaphoreType.DMA((1, lines)),
            pltpu.SemaphoreType.DMA((1, devices)),
        ],
        compiler_params=pltpu.CompilerParams(
            collective_id=1, has_side_effects=True, vmem_limit_bytes=VMEM_LIMIT
        ),
        name="hand_back",
    )(y, order)


def matern(columns, rows):
    squared = None
    for axis in range(3):
        delta = columns[:, axis : axis + 1] - rows[axis : axis + 1, :]
        squared = delta * delta if squared is None else squared + delta * delta
    distance = squared * lax.rsqrt(jnp.maximum(squared, 1e-30))
    rate = ROOT_THREE / LENGTH_SCALE
    rising = KERNEL_GAIN + (KERNEL_GAIN * rate) * distance
    return (rising * jnp.exp2(distance * (-rate * LOG2_E))).astype(jnp.bfloat16)


def near_sums(leaves, v_ref, c_ref, near):
    rows = v_ref.shape[0] // (leaves + 2)
    near[...] = jnp.zeros_like(near)

    def vec_at(slot):
        return pl.ds(pl.multiple_of(slot * rows, rows), rows)

    def coord_at(slot):
        return pl.ds(pl.multiple_of(slot * 8, 8), 8)

    def step(slot, carry):
        here = c_ref[coord_at(slot), :]
        columns = jnp.transpose(here)
        beside = matern(columns, c_ref[coord_at(slot + 1), :])
        within = matern(columns, here)
        x_here = v_ref[vec_at(slot), :]
        x_next = v_ref[vec_at(slot + 1), :]
        near[vec_at(slot + 1), :] += jnp.dot(x_here, beside, preferred_element_type=jnp.float32)
        near[vec_at(slot), :] += jnp.dot(
            x_here, within, preferred_element_type=jnp.float32
        ) + lax.dot_general(
            x_next, beside, (((1,), (1,)), ((), ())), preferred_element_type=jnp.float32
        )
        return carry

    lax.fori_loop(0, leaves + 1, step, 0)


def near_kernel(
    lines,
    leaves,
    v_ref,
    c_ref,
    coef_ref,
    root_ref,
    near_out,
    levels_out,
    roots_out,
    near,
    send_sem,
    recv_sem,
    root_send,
    root_recv,
):
    devices = lines * 2
    nodes = coef_ref.shape[0]
    rows = v_ref.shape[0] // (leaves + 2)
    me = lax.axis_index("leaf") * 2 + lax.axis_index("sub")

    def place(device):
        return {"leaf": device // 2, "sub": lax.rem(device, 2)}

    after = lax.rem(me + 1, devices)
    before = lax.rem(me + devices - 1, devices)
    barrier = pltpu.get_barrier_semaphore()

    def greet(hop, carry):
        pl.semaphore_signal(
            barrier, inc=1, device_id=place(lax.rem(me + hop, devices)), device_id_type=MESH
        )
        return carry

    lax.fori_loop(1, devices, greet, 0)
    pl.semaphore_wait(barrier, devices - 1)

    def root_copy(hop):
        return pltpu.make_async_remote_copy(
            src_ref=root_ref,
            dst_ref=roots_out.at[me],
            send_sem=root_send.at[hop],
            recv_sem=root_recv.at[me],
            device_id=place(lax.rem(me + hop, devices)),
            device_id_type=MESH,
        )

    def start_root(hop, carry):
        root_copy(hop).start()
        return carry

    copies = [
        pltpu.make_async_remote_copy(
            src_ref=coef_ref,
            dst_ref=levels_out.at[which],
            send_sem=send_sem.at[which],
            recv_sem=recv_sem.at[which],
            device_id=place(target),
            device_id_type=MESH,
        )
        for which, target in ((0, after), (2, before))
    ]
    lax.fori_loop(1, devices, start_root, 0)
    for copy in copies:
        copy.start()
    levels_out[1] = coef_ref[...]
    roots_out[me] = root_ref[...]
    near_sums(leaves, v_ref, c_ref, near)
    near_out[...] = near[rows : (leaves + 1) * rows, :]

    def end_root(hop, carry):
        source = lax.rem(me + hop, devices)
        pltpu.make_async_remote_copy(
            src_ref=root_ref,
            dst_ref=roots_out.at[source],
            send_sem=root_send.at[hop],
            recv_sem=root_recv.at[source],
            device_id=place(source),
            device_id_type=MESH,
        ).wait()
        return carry

    lax.fori_loop(1, devices, end_root, 0)
    for copy in copies:
        copy.wait()


def near_and_levels(lines, leaves, v, c, coef, root):
    devices = lines * 2
    rows = v.shape[0] // (leaves + 2)
    return pl.pallas_call(
        functools.partial(near_kernel, lines, leaves),
        out_shape=(
            jax.ShapeDtypeStruct((leaves * rows, v.shape[1]), jnp.float32),
            jax.ShapeDtypeStruct((3,) + coef.shape, jnp.bfloat16),
            jax.ShapeDtypeStruct((devices,) + root.shape, jnp.bfloat16),
        ),
        in_specs=[pl.BlockSpec(memory_space=pltpu.VMEM)] * 4,
        out_specs=(pl.BlockSpec(memory_space=pltpu.VMEM),) * 3,
        scratch_shapes=[
            pltpu.VMEM(v.shape, jnp.float32),
            pltpu.SemaphoreType.DMA((3,)),
            pltpu.SemaphoreType.DMA((3,)),
            pltpu.SemaphoreType.DMA((devices,)),
            pltpu.SemaphoreType.DMA((devices,)),
        ],
        compiler_params=pltpu.CompilerParams(
            collective_id=2, has_side_effects=True, vmem_limit_bytes=VMEM_LIMIT
        ),
        name="near",
    )(v, c, coef, root)


def couple(couplings, gathered_rows):
    return jnp.einsum(
        "gkab,gkvb->gva", couplings, gathered_rows, preferred_element_type=jnp.float32
    )


def on_device(
    vectors,
    coords,
    point_order,
    leaf_basis,
    transfer_local,
    transfer_top,
    partners_local,
    coupling_local,
    top_partners,
    top_coupling,
):
    vec_rows = vectors.shape[0]
    dev_pts = vectors.shape[1]
    subtrees = lax.axis_size(("leaf", "sub"))
    leaves = leaf_basis.shape[0]
    rank_dim = leaf_basis.shape[1]
    leaf_pts = leaf_basis.shape[2]
    node_count = 2 * leaves - 1
    levels = leaves.bit_length()
    partners = partners_local.shape[1]
    top_count = top_partners.shape[1]
    my_index = lax.axis_index(("leaf", "sub"))
    lines = lax.axis_size("leaf")
    fields = jnp.concatenate(
        [
            coords,
            (point_order % leaf_pts)[None].astype(jnp.bfloat16),
            (point_order // leaf_pts % leaves)[None].astype(jnp.bfloat16),
            (point_order // dev_pts)[None].astype(jnp.bfloat16),
            jnp.zeros((FIELDS - 6, dev_pts), jnp.bfloat16),
        ],
        axis=0,
    )
    aux = fields.reshape(FIELDS, dev_pts // CHUNK, CHUNK).transpose(1, 0, 2)
    aux = aux.reshape(FIELDS * dev_pts // CHUNK, CHUNK)
    v_slots, c_slots = arrange(lines, leaves, leaf_pts, vectors, aux)
    leaf_rows = v_slots.reshape(leaves + 2, vec_rows, leaf_pts)[1 : leaves + 1]
    coefficients = jnp.einsum(
        "tvl,tal->tva", leaf_rows, leaf_basis, preferred_element_type=jnp.float32
    ).astype(jnp.bfloat16)
    transfers = transfer_local.reshape(2 * leaves - 2, rank_dim, rank_dim)
    couplings = coupling_local.reshape(node_count, partners, rank_dim, rank_dim)
    per_level = [coefficients]
    offset = 0
    level_count = leaves
    for level_idx in range(levels - 1):
        pair_mats = transfers[offset : offset + level_count].reshape(
            level_count // 2, 2, rank_dim, rank_dim
        )
        pair_coef = per_level[-1].reshape(level_count // 2, 2, vec_rows, rank_dim)
        per_level.append(
            jnp.einsum(
                "icab,icvb->iva", pair_mats, pair_coef, preferred_element_type=jnp.float32
            ).astype(jnp.bfloat16)
        )
        offset = offset + level_count
        level_count = level_count // 2
    all_levels = jnp.concatenate(per_level, axis=0)
    near_part, padded_all, stacked = near_and_levels(
        lines,
        leaves,
        v_slots,
        c_slots,
        all_levels.reshape(node_count * vec_rows, rank_dim),
        per_level[-1].reshape(vec_rows, rank_dim),
    )
    padded_all = padded_all.reshape(3 * node_count, vec_rows, rank_dim)
    local_idx = partners_local - (my_index - 1) * node_count
    local_out = couple(couplings, padded_all[local_idx])
    half_top = subtrees // 2
    quarter_top = subtrees // 4
    top_mats = transfer_top.reshape(subtrees + half_top, rank_dim, rank_dim)
    level_one = jnp.einsum(
        "icab,icvb->iva",
        top_mats[:subtrees].reshape(half_top, 2, rank_dim, rank_dim),
        stacked.reshape(half_top, 2, vec_rows, rank_dim),
        preferred_element_type=jnp.float32,
    ).astype(jnp.bfloat16)
    level_two = jnp.einsum(
        "icab,icvb->iva",
        top_mats[subtrees:].reshape(quarter_top, 2, rank_dim, rank_dim),
        level_one.reshape(quarter_top, 2, vec_rows, rank_dim),
        preferred_element_type=jnp.float32,
    ).astype(jnp.bfloat16)
    top_coef = jnp.concatenate([level_one, level_two], axis=0)
    level_shift = jnp.where(
        jnp.arange(half_top + quarter_top, dtype=jnp.int32)[:, None] >= half_top, half_top, 0
    ).astype(jnp.int32)
    top_out = couple(
        top_coupling.reshape(half_top + quarter_top, top_count, rank_dim, rank_dim),
        top_coef[top_partners + level_shift],
    )
    upper_bar = top_out[half_top:].astype(jnp.bfloat16)
    middle_top = top_out[:half_top] + jnp.einsum(
        "icab,iva->icvb",
        top_mats[subtrees:].reshape(quarter_top, 2, rank_dim, rank_dim),
        upper_bar,
        preferred_element_type=jnp.float32,
    ).reshape(half_top, vec_rows, rank_dim)
    middle_bar = middle_top.astype(jnp.bfloat16)
    mat_mine = lax.dynamic_index_in_dim(top_mats, my_index, 0, keepdims=False)
    parent_mine = lax.dynamic_index_in_dim(middle_bar, my_index // 2, 0, keepdims=False)
    root_down = jnp.einsum("ab,va->vb", mat_mine, parent_mine, preferred_element_type=jnp.float32)
    current = (local_out[node_count - 1] + root_down)[None]
    offset = node_count - 1
    level_count = 1
    for level_idx in range(levels - 1):
        child_count = level_count * 2
        offset = offset - child_count
        pair_mats = transfers[offset : offset + child_count].reshape(
            level_count, 2, rank_dim, rank_dim
        )
        downward = jnp.einsum(
            "icab,iva->icvb",
            pair_mats,
            current.astype(jnp.bfloat16),
            preferred_element_type=jnp.float32,
        ).reshape(child_count, vec_rows, rank_dim)
        current = local_out[offset : offset + child_count] + downward
        level_count = child_count
    far_field = jnp.einsum(
        "tva,tal->tvl", current.astype(jnp.bfloat16), leaf_basis, preferred_element_type=jnp.float32
    )
    answer = (far_field + near_part.reshape(far_field.shape)).astype(jnp.bfloat16)
    return hand_back(
        lines, leaves, answer.reshape(leaves * vec_rows, leaf_pts), point_order.reshape(1, dev_pts)
    )


def solution(mesh):
    in_specs = (
        P(("grp", "vec"), ("leaf", "sub")),
        P("grp", ("leaf", "sub")),
        P(("grp", "leaf", "sub")),
        P(("grp", "leaf", "sub"), None, None),
        P(("grp", "leaf", "sub"), None),
        P("grp", None),
        P(("grp", "leaf", "sub"), None),
        P(("grp", "leaf", "sub"), None, None),
        P("grp", None),
        P("grp", None, None),
    )
    out_specs = P(("grp", "vec"), ("leaf", "sub"))
    return jax.shard_map(
        on_device, mesh=mesh, in_specs=in_specs, out_specs=out_specs, check_vma=False
    )
```

```python
import functools

import jax
import jax.numpy as jnp
from jax import lax
from jax.experimental import pallas as pl
from jax.experimental.pallas import tpu as pltpu
from jax.sharding import PartitionSpec as P

ROOT_THREE = 1.7320508075688772
LENGTH_SCALE = 0.0125
KERNEL_GAIN = 0.25
LOG2_E = 1.4426950408889634
MESH = pl.DeviceIdType.MESH
VMEM_LIMIT = 56 * 1024 * 1024
CHUNK = 1024
FIELDS = 6
AUX_CHUNK = 512


def for_each_block(lines, pairs, sems, process):
    send_sem, pass_sem, recv_sem = sems
    mine = lax.axis_index("leaf")
    core = lax.axis_index("sub")
    other = 1 - core
    barrier = pltpu.get_barrier_semaphore()

    def greet(target):
        pl.semaphore_signal(barrier, inc=1, device_id=target, device_id_type=MESH)

    def copies(block, target, sem):
        return [
            pltpu.make_async_remote_copy(
                src_ref=held.at[block],
                dst_ref=held.at[block],
                send_sem=sem.at[which, block],
                recv_sem=recv_sem.at[which, block],
                device_id=target,
                device_id_type=MESH,
            )
            for which, (own, held) in enumerate(pairs)
        ]

    def ahead(block, way):
        return copies(block, {"leaf": mine + way}, send_sem.at[(way + 1) // 2])

    def across(block):
        return copies(block, {"sub": other}, pass_sem)

    def has(way):
        return mine > 0 if way < 0 else mine < lines - 1

    def guarded(condition, action):
        pl.when(condition)(action)

    def start(some):
        for copy in some:
            copy.start()

    def wait_sent(some):
        for copy in some:
            copy.wait_send()

    def wait_here(some):
        for copy in some:
            copy.wait_recv()

    greet({"sub": other})
    for way in (-1, 1):
        guarded(has(way), lambda way=way: greet({"leaf": mine + way}))
    for own, held in pairs:
        held[mine * 2 + core] = own[...]
    inside = jnp.logical_and(has(-1), has(1))
    guarded(inside, lambda: pl.semaphore_wait(barrier, 3))
    guarded(jnp.logical_not(inside), lambda: pl.semaphore_wait(barrier, 2))

    me = mine * 2 + core
    for way in (-1, 1):
        guarded(has(way), lambda way=way: start(ahead(me, way)))
    start(across(me))
    process(me)
    wait_here(across(mine * 2 + other))
    process(mine * 2 + other)

    def step(hop, carry):
        for way in (-1, 1):
            line = mine - way * hop
            there = line >= 0 if way > 0 else line < lines
            block = line * 2 + core

            def take(way=way, block=block):
                wait_here(across(block))
                guarded(has(way), lambda: start(ahead(block, way)))
                start(across(block))

            guarded(there, take)
        for way in (-1, 1):
            line = mine - way * hop
            there = line >= 0 if way > 0 else line < lines

            def use(line=line):
                process(line * 2 + core)
                wait_here(across(line * 2 + other))
                process(line * 2 + other)

            guarded(there, use)
        return carry

    lax.fori_loop(1, lines, step, 0)

    def finish(line, carry):
        block = line * 2 + core
        wait_sent(across(block))
        for way in (-1, 1):
            upstream = line <= mine if way > 0 else line >= mine
            guarded(
                jnp.logical_and(upstream, has(way)), lambda way=way: wait_sent(ahead(block, way))
            )
        return carry

    lax.fori_loop(0, lines, finish, 0)


def arrange_kernel(
    lines, leaves, x_ref, aux_ref, v_out, c_out, x_all, aux_all, total, send_sem, pass_sem, recv_sem
):
    me = lax.axis_index("leaf") * 2 + lax.axis_index("sub")
    rows = x_ref.shape[0]
    dev_pts = x_ref.shape[1]
    leaf_pts = v_out.shape[1]
    slots = leaves + 2
    slot_pad = -(-slots // 16) * 16
    total[...] = jnp.zeros_like(total)
    slot_ids = lax.broadcasted_iota(jnp.int32, (slot_pad, CHUNK), 0).astype(jnp.bfloat16)
    place_ids = lax.broadcasted_iota(jnp.int32, (leaf_pts, CHUNK), 0).astype(jnp.bfloat16)

    def process(block):
        aux = aux_all[block].astype(jnp.float32)
        for part in range(dev_pts // CHUNK):
            at = part * FIELDS * CHUNK // AUX_CHUNK
            fields = jnp.concatenate(
                [aux[at + k : at + k + FIELDS] for k in range(0, FIELDS * CHUNK // AUX_CHUNK, FIELDS)],
                axis=1,
            )
            x = x_all[block, :, part * CHUNK : (part + 1) * CHUNK]
            slot = (fields[5:6] - me.astype(jnp.float32)) * leaves + fields[4:5] + 1.0
            slot = jnp.clip(slot, -1.0, float(slots)).astype(jnp.bfloat16)
            slot_here = jnp.broadcast_to(slot, (rows, CHUNK))
            zero = jnp.zeros_like(x)
            parts = [jnp.where(slot_here == jnp.bfloat16(k), x, zero) for k in range(slots)]
            chosen = slot_ids == jnp.broadcast_to(slot, (slot_pad, CHUNK))
            for axis in range(3):
                row = fields[axis : axis + 1].astype(jnp.bfloat16)
                row = jnp.broadcast_to(row, (slot_pad, CHUNK))
                parts.append(jnp.where(chosen, row, jnp.zeros_like(row)))
            place = jnp.broadcast_to(fields[3:4].astype(jnp.bfloat16), (leaf_pts, CHUNK))
            one_hot = jnp.where(place_ids == place, jnp.bfloat16(1), jnp.bfloat16(0))
            total[...] += lax.dot_general(
                jnp.concatenate(parts, axis=0),
                one_hot,
                (((1,), (1,)), ((), ())),
                preferred_element_type=jnp.float32,
            ).astype(jnp.bfloat16)

    pairs = ((x_ref, x_all), (aux_ref, aux_all))
    for_each_block(lines, pairs, (send_sem, pass_sem, recv_sem), process)
    v_out[...] = total[: slots * rows, :]
    found = total[slots * rows :, :].astype(jnp.float32)
    c_out[...] = jnp.zeros_like(c_out)
    for slot in range(slots):
        for axis in range(3):
            at = axis * slot_pad + slot
            c_out[slot * 8 + axis : slot * 8 + axis + 1, :] = found[at : at + 1, :]


def arrange(lines, leaves, leaf_pts, x, aux):
    rows, dev_pts = x.shape
    devices = lines * 2
    slots = leaves + 2
    slot_pad = -(-slots // 16) * 16
    return pl.pallas_call(
        functools.partial(arrange_kernel, lines, leaves),
        out_shape=(
            jax.ShapeDtypeStruct((slots * rows, leaf_pts), jnp.bfloat16),
            jax.ShapeDtypeStruct((slots * 8, leaf_pts), jnp.float32),
        ),
        in_specs=[pl.BlockSpec(memory_space=pltpu.VMEM)] * 2,
        out_specs=(pl.BlockSpec(memory_space=pltpu.VMEM),) * 2,
        scratch_shapes=[
            pltpu.VMEM((devices,) + x.shape, jnp.bfloat16),
            pltpu.VMEM((devices,) + aux.shape, jnp.bfloat16),
            pltpu.VMEM((slots * rows + 3 * slot_pad, leaf_pts), jnp.bfloat16),
            pltpu.SemaphoreType.DMA((2, 2, devices)),
            pltpu.SemaphoreType.DMA((2, devices)),
            pltpu.SemaphoreType.DMA((2, devices)),
        ],
        compiler_params=pltpu.CompilerParams(
            collective_id=0, has_side_effects=True, vmem_limit_bytes=VMEM_LIMIT
        ),
        name="arrange",
    )(x, aux)


def hand_back_kernel(
    lines, leaves, y_ref, order_ref, out_ref, y_all, one_hot, leaf_at, send_sem, pass_sem, recv_sem
):
    leaf_pts = y_ref.shape[1]
    rows = y_ref.shape[0] // leaves
    dev_pts = order_ref.shape[1]
    order = order_ref[...]
    leaf_at[...] = (order // leaf_pts).astype(jnp.float32)
    for part in range(dev_pts // CHUNK):
        at = slice(part * CHUNK, (part + 1) * CHUNK)
        place_ids = lax.broadcasted_iota(jnp.int32, (leaf_pts, CHUNK), 0)
        place = jnp.broadcast_to(order[:, at] % leaf_pts, (leaf_pts, CHUNK))
        one_hot[:, at] = jnp.where(place_ids == place, 1.0, 0.0).astype(jnp.bfloat16)
    out_ref[...] = jnp.zeros_like(out_ref)

    def process(block):
        y = y_all[block]

        def chunk(part, carry):
            at = pl.ds(pl.multiple_of(part * CHUNK, CHUNK), CHUNK)
            found = jnp.dot(y, one_hot[:, at], preferred_element_type=jnp.float32)
            leaf = leaf_at[:, at] - (block * leaves).astype(jnp.float32)
            leaf = jnp.clip(leaf, -1.0, float(leaves)).astype(jnp.bfloat16)
            leaf = jnp.broadcast_to(leaf, (rows, CHUNK))
            got = jnp.zeros((rows, CHUNK), jnp.bfloat16)
            for k in range(leaves):
                here = found[k * rows : (k + 1) * rows].astype(jnp.bfloat16)
                got = jnp.where(leaf == jnp.bfloat16(k), here, got)
            out_ref[:, at] += got
            return carry

        lax.fori_loop(0, dev_pts // CHUNK, chunk, 0)

    for_each_block(lines, ((y_ref, y_all),), (send_sem, pass_sem, recv_sem), process)


def hand_back(lines, leaves, y, order):
    devices = lines * 2
    rows = y.shape[0] // leaves
    dev_pts = order.shape[1]
    return pl.pallas_call(
        functools.partial(hand_back_kernel, lines, leaves),
        out_shape=jax.ShapeDtypeStruct((rows, dev_pts), jnp.bfloat16),
        in_specs=[pl.BlockSpec(memory_space=pltpu.VMEM)] * 2,
        out_specs=pl.BlockSpec(memory_space=pltpu.VMEM),
        scratch_shapes=[
            pltpu.VMEM((devices,) + y.shape, jnp.bfloat16),
            pltpu.VMEM((y.shape[1], dev_pts), jnp.bfloat16),
            pltpu.VMEM((1, dev_pts), jnp.float32),
            pltpu.SemaphoreType.DMA((2, 1, devices)),
            pltpu.SemaphoreType.DMA((1, devices)),
            pltpu.SemaphoreType.DMA((1, devices)),
        ],
        compiler_params=pltpu.CompilerParams(
            collective_id=1, has_side_effects=True, vmem_limit_bytes=VMEM_LIMIT
        ),
        name="hand_back",
    )(y, order)


def matern(columns, rows):
    squared = None
    for axis in range(3):
        delta = columns[:, axis : axis + 1] - rows[axis : axis + 1, :]
        squared = delta * delta if squared is None else squared + delta * delta
    distance = squared * lax.rsqrt(jnp.maximum(squared, 1e-30))
    rate = ROOT_THREE / LENGTH_SCALE
    rising = KERNEL_GAIN + (KERNEL_GAIN * rate) * distance
    return (rising * jnp.exp2(distance * (-rate * LOG2_E))).astype(jnp.bfloat16)


def near_sums(leaves, v_ref, c_ref, near):
    rows = v_ref.shape[0] // (leaves + 2)
    near[...] = jnp.zeros_like(near)

    def vec_at(slot):
        return pl.ds(pl.multiple_of(slot * rows, rows), rows)

    def coord_at(slot):
        return pl.ds(pl.multiple_of(slot * 8, 8), 8)

    def step(slot, carry):
        here = c_ref[coord_at(slot), :]
        columns = jnp.transpose(here)
        beside = matern(columns, c_ref[coord_at(slot + 1), :])
        within = matern(columns, here)
        x_here = v_ref[vec_at(slot), :]
        x_next = v_ref[vec_at(slot + 1), :]
        near[vec_at(slot + 1), :] += jnp.dot(x_here, beside, preferred_element_type=jnp.float32)
        near[vec_at(slot), :] += jnp.dot(
            x_here, within, preferred_element_type=jnp.float32
        ) + lax.dot_general(
            x_next, beside, (((1,), (1,)), ((), ())), preferred_element_type=jnp.float32
        )
        return carry

    lax.fori_loop(0, leaves + 1, step, 0)


def near_kernel(
    lines,
    leaves,
    v_ref,
    c_ref,
    coef_ref,
    root_ref,
    near_out,
    levels_out,
    roots_out,
    near,
    send_sem,
    recv_sem,
    root_send,
    root_recv,
):
    devices = lines * 2
    nodes = coef_ref.shape[0]
    rows = v_ref.shape[0] // (leaves + 2)
    me = lax.axis_index("leaf") * 2 + lax.axis_index("sub")

    def place(device):
        return {"leaf": device // 2, "sub": lax.rem(device, 2)}

    after = lax.rem(me + 1, devices)
    before = lax.rem(me + devices - 1, devices)
    barrier = pltpu.get_barrier_semaphore()

    def greet(hop, carry):
        pl.semaphore_signal(
            barrier, inc=1, device_id=place(lax.rem(me + hop, devices)), device_id_type=MESH
        )
        return carry

    lax.fori_loop(1, devices, greet, 0)
    pl.semaphore_wait(barrier, devices - 1)

    def root_copy(hop):
        return pltpu.make_async_remote_copy(
            src_ref=root_ref,
            dst_ref=roots_out.at[me],
            send_sem=root_send.at[hop],
            recv_sem=root_recv.at[me],
            device_id=place(lax.rem(me + hop, devices)),
            device_id_type=MESH,
        )

    def start_root(hop, carry):
        root_copy(hop).start()
        return carry

    copies = [
        pltpu.make_async_remote_copy(
            src_ref=coef_ref,
            dst_ref=levels_out.at[which],
            send_sem=send_sem.at[which],
            recv_sem=recv_sem.at[which],
            device_id=place(target),
            device_id_type=MESH,
        )
        for which, target in ((0, after), (2, before))
    ]
    lax.fori_loop(1, devices, start_root, 0)
    for copy in copies:
        copy.start()
    levels_out[1] = coef_ref[...]
    roots_out[me] = root_ref[...]
    near_sums(leaves, v_ref, c_ref, near)
    near_out[...] = near[rows : (leaves + 1) * rows, :]

    def end_root(hop, carry):
        source = lax.rem(me + hop, devices)
        pltpu.make_async_remote_copy(
            src_ref=root_ref,
            dst_ref=roots_out.at[source],
            send_sem=root_send.at[hop],
            recv_sem=root_recv.at[source],
            device_id=place(source),
            device_id_type=MESH,
        ).wait()
        return carry

    lax.fori_loop(1, devices, end_root, 0)
    for copy in copies:
        copy.wait()


def near_and_levels(lines, leaves, v, c, coef, root):
    devices = lines * 2
    rows = v.shape[0] // (leaves + 2)
    return pl.pallas_call(
        functools.partial(near_kernel, lines, leaves),
        out_shape=(
            jax.ShapeDtypeStruct((leaves * rows, v.shape[1]), jnp.float32),
            jax.ShapeDtypeStruct((3,) + coef.shape, jnp.bfloat16),
            jax.ShapeDtypeStruct((devices,) + root.shape, jnp.bfloat16),
        ),
        in_specs=[pl.BlockSpec(memory_space=pltpu.VMEM)] * 4,
        out_specs=(pl.BlockSpec(memory_space=pltpu.VMEM),) * 3,
        scratch_shapes=[
            pltpu.VMEM(v.shape, jnp.float32),
            pltpu.SemaphoreType.DMA((3,)),
            pltpu.SemaphoreType.DMA((3,)),
            pltpu.SemaphoreType.DMA((devices,)),
            pltpu.SemaphoreType.DMA((devices,)),
        ],
        compiler_params=pltpu.CompilerParams(
            collective_id=2, has_side_effects=True, vmem_limit_bytes=VMEM_LIMIT
        ),
        name="near",
    )(v, c, coef, root)


def couple(couplings, gathered_rows):
    return jnp.einsum(
        "gkab,gkvb->gva", couplings, gathered_rows, preferred_element_type=jnp.float32
    )


def on_device(
    vectors,
    coords,
    point_order,
    leaf_basis,
    transfer_local,
    transfer_top,
    partners_local,
    coupling_local,
    top_partners,
    top_coupling,
):
    vec_rows = vectors.shape[0]
    dev_pts = vectors.shape[1]
    subtrees = lax.axis_size(("leaf", "sub"))
    leaves = leaf_basis.shape[0]
    rank_dim = leaf_basis.shape[1]
    leaf_pts = leaf_basis.shape[2]
    node_count = 2 * leaves - 1
    levels = leaves.bit_length()
    partners = partners_local.shape[1]
    top_count = top_partners.shape[1]
    my_index = lax.axis_index(("leaf", "sub"))
    lines = lax.axis_size("leaf")
    fields = jnp.concatenate(
        [
            coords,
            (point_order % leaf_pts)[None].astype(jnp.bfloat16),
            (point_order // leaf_pts % leaves)[None].astype(jnp.bfloat16),
            (point_order // dev_pts)[None].astype(jnp.bfloat16),
        ],
        axis=0,
    )
    aux = fields.reshape(FIELDS, dev_pts // AUX_CHUNK, AUX_CHUNK).transpose(1, 0, 2)
    aux = aux.reshape(FIELDS * dev_pts // AUX_CHUNK, AUX_CHUNK)
    v_slots, c_slots = arrange(lines, leaves, leaf_pts, vectors, aux)
    leaf_rows = v_slots.reshape(leaves + 2, vec_rows, leaf_pts)[1 : leaves + 1]
    coefficients = jnp.einsum(
        "tvl,tal->tva", leaf_rows, leaf_basis, preferred_element_type=jnp.float32
    ).astype(jnp.bfloat16)
    transfers = transfer_local.reshape(2 * leaves - 2, rank_dim, rank_dim)
    couplings = coupling_local.reshape(node_count, partners, rank_dim, rank_dim)
    per_level = [coefficients]
    offset = 0
    level_count = leaves
    for level_idx in range(levels - 1):
        pair_mats = transfers[offset : offset + level_count].reshape(
            level_count // 2, 2, rank_dim, rank_dim
        )
        pair_coef = per_level[-1].reshape(level_count // 2, 2, vec_rows, rank_dim)
        per_level.append(
            jnp.einsum(
                "icab,icvb->iva", pair_mats, pair_coef, preferred_element_type=jnp.float32
            ).astype(jnp.bfloat16)
        )
        offset = offset + level_count
        level_count = level_count // 2
    all_levels = jnp.concatenate(per_level, axis=0)
    near_part, padded_all, stacked = near_and_levels(
        lines,
        leaves,
        v_slots,
        c_slots,
        all_levels.reshape(node_count * vec_rows, rank_dim),
        per_level[-1].reshape(vec_rows, rank_dim),
    )
    padded_all = padded_all.reshape(3 * node_count, vec_rows, rank_dim)
    local_idx = partners_local - (my_index - 1) * node_count
    local_out = couple(couplings, padded_all[local_idx])
    half_top = subtrees // 2
    quarter_top = subtrees // 4
    top_mats = transfer_top.reshape(subtrees + half_top, rank_dim, rank_dim)
    level_one = jnp.einsum(
        "icab,icvb->iva",
        top_mats[:subtrees].reshape(half_top, 2, rank_dim, rank_dim),
        stacked.reshape(half_top, 2, vec_rows, rank_dim),
        preferred_element_type=jnp.float32,
    ).astype(jnp.bfloat16)
    level_two = jnp.einsum(
        "icab,icvb->iva",
        top_mats[subtrees:].reshape(quarter_top, 2, rank_dim, rank_dim),
        level_one.reshape(quarter_top, 2, vec_rows, rank_dim),
        preferred_element_type=jnp.float32,
    ).astype(jnp.bfloat16)
    top_coef = jnp.concatenate([level_one, level_two], axis=0)
    level_shift = jnp.where(
        jnp.arange(half_top + quarter_top, dtype=jnp.int32)[:, None] >= half_top, half_top, 0
    ).astype(jnp.int32)
    top_out = couple(
        top_coupling.reshape(half_top + quarter_top, top_count, rank_dim, rank_dim),
        top_coef[top_partners + level_shift],
    )
    upper_bar = top_out[half_top:].astype(jnp.bfloat16)
    middle_top = top_out[:half_top] + jnp.einsum(
        "icab,iva->icvb",
        top_mats[subtrees:].reshape(quarter_top, 2, rank_dim, rank_dim),
        upper_bar,
        preferred_element_type=jnp.float32,
    ).reshape(half_top, vec_rows, rank_dim)
    middle_bar = middle_top.astype(jnp.bfloat16)
    mat_mine = lax.dynamic_index_in_dim(top_mats, my_index, 0, keepdims=False)
    parent_mine = lax.dynamic_index_in_dim(middle_bar, my_index // 2, 0, keepdims=False)
    root_down = jnp.einsum("ab,va->vb", mat_mine, parent_mine, preferred_element_type=jnp.float32)
    current = (local_out[node_count - 1] + root_down)[None]
    offset = node_count - 1
    level_count = 1
    for level_idx in range(levels - 1):
        child_count = level_count * 2
        offset = offset - child_count
        pair_mats = transfers[offset : offset + child_count].reshape(
            level_count, 2, rank_dim, rank_dim
        )
        downward = jnp.einsum(
            "icab,iva->icvb",
            pair_mats,
            current.astype(jnp.bfloat16),
            preferred_element_type=jnp.float32,
        ).reshape(child_count, vec_rows, rank_dim)
        current = local_out[offset : offset + child_count] + downward
        level_count = child_count
    far_field = jnp.einsum(
        "tva,tal->tvl", current.astype(jnp.bfloat16), leaf_basis, preferred_element_type=jnp.float32
    )
    answer = (far_field + near_part.reshape(far_field.shape)).astype(jnp.bfloat16)
    return hand_back(
        lines, leaves, answer.reshape(leaves * vec_rows, leaf_pts), point_order.reshape(1, dev_pts)
    )


def solution(mesh):
    in_specs = (
        P(("grp", "vec"), ("leaf", "sub")),
        P("grp", ("leaf", "sub")),
        P(("grp", "leaf", "sub")),
        P(("grp", "leaf", "sub"), None, None),
        P(("grp", "leaf", "sub"), None),
        P("grp", None),
        P(("grp", "leaf", "sub"), None),
        P(("grp", "leaf", "sub"), None, None),
        P("grp", None),
        P("grp", None, None),
    )
    out_specs = P(("grp", "vec"), ("leaf", "sub"))
    return jax.shard_map(
        on_device, mesh=mesh, in_specs=in_specs, out_specs=out_specs, check_vma=False
    )
```

```python
import functools

import jax
import jax.numpy as jnp
from jax import lax
from jax.experimental import pallas as pl
from jax.experimental.pallas import tpu as pltpu
from jax.sharding import PartitionSpec as P

ROOT_THREE = 1.7320508075688772
LENGTH_SCALE = 0.0125
KERNEL_GAIN = 0.25
LOG2_E = 1.4426950408889634
MESH = pl.DeviceIdType.MESH
VMEM_LIMIT = 56 * 1024 * 1024
CHUNK = 1024
FIELDS = 6
AUX_CHUNK = 512


def cut_rows(rows):
    return rows // 2 if rows % 32 == 0 else rows


def piece_count(arrays):
    return sum(a.shape[0] // cut_rows(a.shape[0]) for a in arrays)


def for_each_block(lines, pairs, sems, process, prepare):
    send_sem, pass_sem, recv_sem = sems
    mine = lax.axis_index("leaf")
    core = lax.axis_index("sub")
    other = 1 - core
    barrier = pltpu.get_barrier_semaphore()

    def greet(target):
        pl.semaphore_signal(barrier, inc=1, device_id=target, device_id_type=MESH)

    pieces = []
    for own, held in pairs:
        cut = cut_rows(own.shape[0])
        pieces += [(held, pl.ds(at, cut)) for at in range(0, own.shape[0], cut)]

    def copies(block, target, sem):
        return [
            pltpu.make_async_remote_copy(
                src_ref=held.at[block, rows],
                dst_ref=held.at[block, rows],
                send_sem=sem.at[which, block],
                recv_sem=recv_sem.at[which, block],
                device_id=target,
                device_id_type=MESH,
            )
            for which, (held, rows) in enumerate(pieces)
        ]

    def ahead(block, way):
        return copies(block, {"leaf": mine + way}, send_sem.at[(way + 1) // 2])

    def across(block):
        return copies(block, {"sub": other}, pass_sem)

    def has(way):
        return mine > 0 if way < 0 else mine < lines - 1

    def guarded(condition, action):
        pl.when(condition)(action)

    def start(some):
        for copy in some:
            copy.start()

    def wait_sent(some):
        for copy in some:
            copy.wait_send()

    def wait_here(some):
        for copy in some:
            copy.wait_recv()

    greet({"sub": other})
    for way in (-1, 1):
        guarded(has(way), lambda way=way: greet({"leaf": mine + way}))
    for own, held in pairs:
        held[mine * 2 + core] = own[...]
    inside = jnp.logical_and(has(-1), has(1))
    guarded(inside, lambda: pl.semaphore_wait(barrier, 3))
    guarded(jnp.logical_not(inside), lambda: pl.semaphore_wait(barrier, 2))

    me = mine * 2 + core
    for way in (-1, 1):
        guarded(has(way), lambda way=way: start(ahead(me, way)))
    start(across(me))
    prepare()
    process(me)
    wait_here(across(mine * 2 + other))
    process(mine * 2 + other)

    def step(hop, carry):
        for way in (-1, 1):
            line = mine - way * hop
            there = line >= 0 if way > 0 else line < lines
            block = line * 2 + core

            def take(way=way, block=block):
                for which, passed in enumerate(across(block)):
                    passed.wait_recv()
                    guarded(has(way), lambda which=which: ahead(block, way)[which].start())
                    passed.start()

            guarded(there, take)
        for way in (-1, 1):
            line = mine - way * hop
            there = line >= 0 if way > 0 else line < lines

            def use(line=line):
                process(line * 2 + core)
                wait_here(across(line * 2 + other))
                process(line * 2 + other)

            guarded(there, use)
        return carry

    lax.fori_loop(1, lines, step, 0)

    def finish(line, carry):
        block = line * 2 + core
        wait_sent(across(block))
        for way in (-1, 1):
            upstream = line <= mine if way > 0 else line >= mine
            guarded(
                jnp.logical_and(upstream, has(way)), lambda way=way: wait_sent(ahead(block, way))
            )
        return carry

    lax.fori_loop(0, lines, finish, 0)


def arrange_kernel(
    lines, leaves, x_ref, aux_ref, v_out, c_out, x_all, aux_all, total, send_sem, pass_sem, recv_sem
):
    me = lax.axis_index("leaf") * 2 + lax.axis_index("sub")
    rows = x_ref.shape[0]
    dev_pts = x_ref.shape[1]
    leaf_pts = v_out.shape[1]
    slots = leaves + 2
    slot_pad = -(-slots // 16) * 16

    def prepare():
        total[...] = jnp.zeros_like(total)

    slot_ids = lax.broadcasted_iota(jnp.int32, (slot_pad, CHUNK), 0).astype(jnp.bfloat16)
    place_ids = lax.broadcasted_iota(jnp.int32, (leaf_pts, CHUNK), 0).astype(jnp.bfloat16)

    def process(block):
        aux = aux_all[block].astype(jnp.float32)
        for part in range(dev_pts // CHUNK):
            at = part * FIELDS * CHUNK // AUX_CHUNK
            fields = jnp.concatenate(
                [aux[at + k : at + k + FIELDS] for k in range(0, FIELDS * CHUNK // AUX_CHUNK, FIELDS)],
                axis=1,
            )
            x = x_all[block, :, part * CHUNK : (part + 1) * CHUNK]
            slot = (fields[5:6] - me.astype(jnp.float32)) * leaves + fields[4:5] + 1.0
            slot = jnp.clip(slot, -1.0, float(slots)).astype(jnp.bfloat16)
            slot_here = jnp.broadcast_to(slot, (rows, CHUNK))
            zero = jnp.zeros_like(x)
            parts = [jnp.where(slot_here == jnp.bfloat16(k), x, zero) for k in range(slots)]
            chosen = slot_ids == jnp.broadcast_to(slot, (slot_pad, CHUNK))
            for axis in range(3):
                row = fields[axis : axis + 1].astype(jnp.bfloat16)
                row = jnp.broadcast_to(row, (slot_pad, CHUNK))
                parts.append(jnp.where(chosen, row, jnp.zeros_like(row)))
            place = jnp.broadcast_to(fields[3:4].astype(jnp.bfloat16), (leaf_pts, CHUNK))
            one_hot = jnp.where(place_ids == place, jnp.bfloat16(1), jnp.bfloat16(0))
            total[...] += lax.dot_general(
                jnp.concatenate(parts, axis=0),
                one_hot,
                (((1,), (1,)), ((), ())),
                preferred_element_type=jnp.float32,
            ).astype(jnp.bfloat16)

    pairs = ((x_ref, x_all), (aux_ref, aux_all))
    for_each_block(lines, pairs, (send_sem, pass_sem, recv_sem), process, prepare)
    v_out[...] = total[: slots * rows, :]
    found = total[slots * rows :, :].astype(jnp.float32)
    c_out[...] = jnp.zeros_like(c_out)
    for slot in range(slots):
        for axis in range(3):
            at = axis * slot_pad + slot
            c_out[slot * 8 + axis : slot * 8 + axis + 1, :] = found[at : at + 1, :]


def arrange(lines, leaves, leaf_pts, x, aux):
    rows, dev_pts = x.shape
    devices = lines * 2
    slots = leaves + 2
    slot_pad = -(-slots // 16) * 16
    return pl.pallas_call(
        functools.partial(arrange_kernel, lines, leaves),
        out_shape=(
            jax.ShapeDtypeStruct((slots * rows, leaf_pts), jnp.bfloat16),
            jax.ShapeDtypeStruct((slots * 8, leaf_pts), jnp.float32),
        ),
        in_specs=[pl.BlockSpec(memory_space=pltpu.VMEM)] * 2,
        out_specs=(pl.BlockSpec(memory_space=pltpu.VMEM),) * 2,
        scratch_shapes=[
            pltpu.VMEM((devices,) + x.shape, jnp.bfloat16),
            pltpu.VMEM((devices,) + aux.shape, jnp.bfloat16),
            pltpu.VMEM((slots * rows + 3 * slot_pad, leaf_pts), jnp.bfloat16),
            pltpu.SemaphoreType.DMA((2, piece_count([x, aux]), devices)),
            pltpu.SemaphoreType.DMA((piece_count([x, aux]), devices)),
            pltpu.SemaphoreType.DMA((piece_count([x, aux]), devices)),
        ],
        compiler_params=pltpu.CompilerParams(
            collective_id=0, has_side_effects=True, vmem_limit_bytes=VMEM_LIMIT
        ),
        name="arrange",
    )(x, aux)


def hand_back_kernel(
    lines, leaves, y_ref, order_ref, out_ref, y_all, one_hot, leaf_at, send_sem, pass_sem, recv_sem
):
    leaf_pts = y_ref.shape[1]
    rows = y_ref.shape[0] // leaves
    dev_pts = order_ref.shape[1]

    def prepare():
        place_ids = lax.broadcasted_iota(jnp.int32, (leaf_pts, CHUNK), 0).astype(jnp.bfloat16)
        for part in range(dev_pts // CHUNK):
            at = slice(part * CHUNK, (part + 1) * CHUNK)
            order = order_ref[:, at]
            leaf_at[:, at] = (order // leaf_pts).astype(jnp.float32)
            place = (order % leaf_pts).astype(jnp.float32).astype(jnp.bfloat16)
            place = jnp.broadcast_to(place, (leaf_pts, CHUNK))
            one_hot[:, at] = jnp.where(place_ids == place, jnp.bfloat16(1), jnp.bfloat16(0))
        out_ref[...] = jnp.zeros_like(out_ref)

    def process(block):
        y = y_all[block]

        def chunk(part, carry):
            at = pl.ds(pl.multiple_of(part * CHUNK, CHUNK), CHUNK)
            found = jnp.dot(y, one_hot[:, at], preferred_element_type=jnp.float32)
            leaf = leaf_at[:, at] - (block * leaves).astype(jnp.float32)
            leaf = jnp.clip(leaf, -1.0, float(leaves)).astype(jnp.bfloat16)
            leaf = jnp.broadcast_to(leaf, (rows, CHUNK))
            got = jnp.zeros((rows, CHUNK), jnp.bfloat16)
            for k in range(leaves):
                here = found[k * rows : (k + 1) * rows].astype(jnp.bfloat16)
                got = jnp.where(leaf == jnp.bfloat16(k), here, got)
            out_ref[:, at] += got
            return carry

        lax.fori_loop(0, dev_pts // CHUNK, chunk, 0)

    sems = (send_sem, pass_sem, recv_sem)
    for_each_block(lines, ((y_ref, y_all),), sems, process, prepare)


def hand_back(lines, leaves, y, order):
    devices = lines * 2
    rows = y.shape[0] // leaves
    dev_pts = order.shape[1]
    return pl.pallas_call(
        functools.partial(hand_back_kernel, lines, leaves),
        out_shape=jax.ShapeDtypeStruct((rows, dev_pts), jnp.bfloat16),
        in_specs=[pl.BlockSpec(memory_space=pltpu.VMEM)] * 2,
        out_specs=pl.BlockSpec(memory_space=pltpu.VMEM),
        scratch_shapes=[
            pltpu.VMEM((devices,) + y.shape, jnp.bfloat16),
            pltpu.VMEM((y.shape[1], dev_pts), jnp.bfloat16),
            pltpu.VMEM((1, dev_pts), jnp.float32),
            pltpu.SemaphoreType.DMA((2, piece_count([y]), devices)),
            pltpu.SemaphoreType.DMA((piece_count([y]), devices)),
            pltpu.SemaphoreType.DMA((piece_count([y]), devices)),
        ],
        compiler_params=pltpu.CompilerParams(
            collective_id=1, has_side_effects=True, vmem_limit_bytes=VMEM_LIMIT
        ),
        name="hand_back",
    )(y, order)


def matern(columns, rows):
    squared = None
    for axis in range(3):
        delta = columns[:, axis : axis + 1] - rows[axis : axis + 1, :]
        squared = delta * delta if squared is None else squared + delta * delta
    distance = squared * lax.rsqrt(jnp.maximum(squared, 1e-30))
    rate = ROOT_THREE / LENGTH_SCALE
    rising = KERNEL_GAIN + (KERNEL_GAIN * rate) * distance
    return (rising * jnp.exp2(distance * (-rate * LOG2_E))).astype(jnp.bfloat16)


def near_sums(leaves, v_ref, c_ref, near):
    rows = v_ref.shape[0] // (leaves + 2)
    near[...] = jnp.zeros_like(near)

    def vec_at(slot):
        return pl.ds(pl.multiple_of(slot * rows, rows), rows)

    def coord_at(slot):
        return pl.ds(pl.multiple_of(slot * 8, 8), 8)

    def step(slot, carry):
        here = c_ref[coord_at(slot), :]
        columns = jnp.transpose(here)
        beside = matern(columns, c_ref[coord_at(slot + 1), :])
        within = matern(columns, here)
        x_here = v_ref[vec_at(slot), :]
        x_next = v_ref[vec_at(slot + 1), :]
        near[vec_at(slot + 1), :] += jnp.dot(x_here, beside, preferred_element_type=jnp.float32)
        near[vec_at(slot), :] += jnp.dot(
            x_here, within, preferred_element_type=jnp.float32
        ) + lax.dot_general(
            x_next, beside, (((1,), (1,)), ((), ())), preferred_element_type=jnp.float32
        )
        return carry

    lax.fori_loop(0, leaves + 1, step, 0)


def near_kernel(
    lines,
    leaves,
    v_ref,
    c_ref,
    coef_ref,
    root_ref,
    near_out,
    levels,
    roots_out,
    near,
    send_sem,
    recv_sem,
    root_send,
    root_recv,
):
    devices = lines * 2
    nodes = coef_ref.shape[0]
    rows = v_ref.shape[0] // (leaves + 2)
    me = lax.axis_index("leaf") * 2 + lax.axis_index("sub")

    def place(device):
        return {"leaf": device // 2, "sub": lax.rem(device, 2)}

    after = lax.rem(me + 1, devices)
    before = lax.rem(me + devices - 1, devices)
    barrier = pltpu.get_barrier_semaphore()

    def greet(hop, carry):
        pl.semaphore_signal(
            barrier, inc=1, device_id=place(lax.rem(me + hop, devices)), device_id_type=MESH
        )
        return carry

    lax.fori_loop(1, devices, greet, 0)
    pl.semaphore_wait(barrier, devices - 1)

    def root_copy(hop):
        return pltpu.make_async_remote_copy(
            src_ref=root_ref,
            dst_ref=roots_out.at[me],
            send_sem=root_send.at[hop],
            recv_sem=root_recv.at[me],
            device_id=place(lax.rem(me + hop, devices)),
            device_id_type=MESH,
        )

    def start_root(hop, carry):
        root_copy(hop).start()
        return carry

    copies = [
        pltpu.make_async_remote_copy(
            src_ref=coef_ref,
            dst_ref=levels.at[which],
            send_sem=send_sem.at[which],
            recv_sem=recv_sem.at[which],
            device_id=place(target),
            device_id_type=MESH,
        )
        for which, target in ((0, after), (2, before))
    ]
    lax.fori_loop(1, devices, start_root, 0)
    for copy in copies:
        copy.start()
    levels[1] = coef_ref[...]
    roots_out[me] = root_ref[...]
    near_sums(leaves, v_ref, c_ref, near)
    near_out[...] = near[rows : (leaves + 1) * rows, :]

    def end_root(hop, carry):
        source = lax.rem(me + hop, devices)
        pltpu.make_async_remote_copy(
            src_ref=root_ref,
            dst_ref=roots_out.at[source],
            send_sem=root_send.at[hop],
            recv_sem=root_recv.at[source],
            device_id=place(source),
            device_id_type=MESH,
        ).wait()
        return carry

    lax.fori_loop(1, devices, end_root, 0)
    for copy in copies:
        copy.wait()


def couple_kernel(rows, levels, weight_ref, partner_ref, coupled_out, weights):
    pairs_total = weight_ref.shape[0]
    rank_dim = levels.shape[1]
    pair_rows = rank_dim // 2
    for k in range(pair_rows):
        part = weight_ref[:, k * 2 * rank_dim : (k + 1) * 2 * rank_dim]
        weights[k * pairs_total : (k + 1) * pairs_total, :] = part.astype(jnp.float32)

    node_total = coupled_out.shape[0] // rows
    partners = pairs_total // node_total
    mixed = lax.broadcasted_iota(jnp.int32, (rank_dim, rank_dim), 0)
    wanted = lax.broadcasted_iota(jnp.int32, (rank_dim, rank_dim), 1)
    even = jnp.logical_and(mixed < pair_rows, wanted == 2 * mixed)
    odd = jnp.logical_and(mixed >= pair_rows, wanted == 2 * (mixed - pair_rows) + 1)
    unmix = jnp.where(jnp.logical_or(even, odd), 1.0, 0.0).astype(jnp.bfloat16)

    def node(index, carry):
        low = jnp.zeros((rows, pair_rows), jnp.float32)
        high = jnp.zeros((rows, pair_rows), jnp.float32)
        for k in range(partners):
            pair = index * partners + k
            matrix = weights[pl.ds(pair, pair_rows, stride=pairs_total), :].astype(jnp.bfloat16)
            number = partner_ref[pair]
            x = levels[pl.ds(pl.multiple_of(number * rows, rows), rows), :]
            dims = (((1,), (1,)), ((), ()))
            low += lax.dot_general(
                x, matrix[:, :rank_dim], dims, preferred_element_type=jnp.float32
            )
            high += lax.dot_general(
                x, matrix[:, rank_dim:], dims, preferred_element_type=jnp.float32
            )
        both = jnp.concatenate([low, high], axis=1)
        coupled_out[pl.ds(pl.multiple_of(index * rows, rows), rows), :] = both
        return carry

    lax.fori_loop(0, node_total, node, 0)
    both = coupled_out[...]
    upper = both.astype(jnp.bfloat16)
    lower = (both - upper.astype(jnp.float32)).astype(jnp.bfloat16)
    coupled_out[...] = jnp.dot(upper, unmix, preferred_element_type=jnp.float32) + jnp.dot(
        lower, unmix, preferred_element_type=jnp.float32
    )


def couple_local(rows, levels, weights, partners):
    pairs_total, entries = weights.shape
    rank_dim = levels.shape[1]
    return pl.pallas_call(
        functools.partial(couple_kernel, rows),
        out_shape=jax.ShapeDtypeStruct((levels.shape[0] // 3, rank_dim), jnp.float32),
        in_specs=[
            pl.BlockSpec(memory_space=pltpu.VMEM),
            pl.BlockSpec(memory_space=pltpu.VMEM),
            pl.BlockSpec(memory_space=pltpu.SMEM),
        ],
        out_specs=pl.BlockSpec(memory_space=pltpu.VMEM),
        scratch_shapes=[
            pltpu.VMEM((pairs_total * entries // (2 * rank_dim), 2 * rank_dim), jnp.float32)
        ],
        compiler_params=pltpu.CompilerParams(vmem_limit_bytes=VMEM_LIMIT),
        name="couple",
    )(levels, weights, partners)


def near_and_levels(lines, leaves, v, c, coef, root):
    devices = lines * 2
    rows = v.shape[0] // (leaves + 2)
    return pl.pallas_call(
        functools.partial(near_kernel, lines, leaves),
        out_shape=(
            jax.ShapeDtypeStruct((leaves * rows, v.shape[1]), jnp.float32),
            jax.ShapeDtypeStruct((3,) + coef.shape, jnp.bfloat16),
            jax.ShapeDtypeStruct((devices,) + root.shape, jnp.bfloat16),
        ),
        in_specs=[pl.BlockSpec(memory_space=pltpu.VMEM)] * 4,
        out_specs=(pl.BlockSpec(memory_space=pltpu.VMEM),) * 3,
        scratch_shapes=[
            pltpu.VMEM(v.shape, jnp.float32),
            pltpu.SemaphoreType.DMA((3,)),
            pltpu.SemaphoreType.DMA((3,)),
            pltpu.SemaphoreType.DMA((devices,)),
            pltpu.SemaphoreType.DMA((devices,)),
        ],
        compiler_params=pltpu.CompilerParams(
            collective_id=2, has_side_effects=True, vmem_limit_bytes=VMEM_LIMIT
        ),
        name="near",
    )(v, c, coef, root)


def couple(couplings, gathered_rows):
    return jnp.einsum(
        "gkab,gkvb->gva", couplings, gathered_rows, preferred_element_type=jnp.float32
    )


def on_device(
    vectors,
    coords,
    point_order,
    leaf_basis,
    transfer_local,
    transfer_top,
    partners_local,
    coupling_local,
    top_partners,
    top_coupling,
):
    vec_rows = vectors.shape[0]
    dev_pts = vectors.shape[1]
    subtrees = lax.axis_size(("leaf", "sub"))
    leaves = leaf_basis.shape[0]
    rank_dim = leaf_basis.shape[1]
    leaf_pts = leaf_basis.shape[2]
    node_count = 2 * leaves - 1
    levels = leaves.bit_length()
    partners = partners_local.shape[1]
    top_count = top_partners.shape[1]
    my_index = lax.axis_index(("leaf", "sub"))
    lines = lax.axis_size("leaf")
    fields = jnp.concatenate(
        [
            coords,
            (point_order % leaf_pts)[None].astype(jnp.bfloat16),
            (point_order // leaf_pts % leaves)[None].astype(jnp.bfloat16),
            (point_order // dev_pts)[None].astype(jnp.bfloat16),
        ],
        axis=0,
    )
    aux = fields.reshape(FIELDS, dev_pts // AUX_CHUNK, AUX_CHUNK).transpose(1, 0, 2)
    aux = aux.reshape(FIELDS * dev_pts // AUX_CHUNK, AUX_CHUNK)
    v_slots, c_slots = arrange(lines, leaves, leaf_pts, vectors, aux)
    leaf_rows = v_slots.reshape(leaves + 2, vec_rows, leaf_pts)[1 : leaves + 1]
    coefficients = jnp.einsum(
        "tvl,tal->tva", leaf_rows, leaf_basis, preferred_element_type=jnp.float32
    ).astype(jnp.bfloat16)
    transfers = transfer_local.reshape(2 * leaves - 2, rank_dim, rank_dim)
    per_level = [coefficients]
    offset = 0
    level_count = leaves
    for level_idx in range(levels - 1):
        pair_mats = transfers[offset : offset + level_count].reshape(
            level_count // 2, 2, rank_dim, rank_dim
        )
        pair_coef = per_level[-1].reshape(level_count // 2, 2, vec_rows, rank_dim)
        per_level.append(
            jnp.einsum(
                "icab,icvb->iva", pair_mats, pair_coef, preferred_element_type=jnp.float32
            ).astype(jnp.bfloat16)
        )
        offset = offset + level_count
        level_count = level_count // 2
    all_levels = jnp.concatenate(per_level, axis=0)
    local_idx = partners_local - (my_index - 1) * node_count
    near_part, padded_all, stacked = near_and_levels(
        lines,
        leaves,
        v_slots,
        c_slots,
        all_levels.reshape(node_count * vec_rows, rank_dim),
        per_level[-1].reshape(vec_rows, rank_dim),
    )
    local_out = couple_local(
        vec_rows,
        padded_all.reshape(3 * node_count * vec_rows, rank_dim),
        coupling_local.reshape(node_count * partners, rank_dim * rank_dim),
        local_idx.reshape(node_count * partners),
    )
    local_out = local_out.reshape(node_count, vec_rows, rank_dim)
    stacked = stacked.reshape(subtrees, vec_rows, rank_dim)
    half_top = subtrees // 2
    quarter_top = subtrees // 4
    top_mats = transfer_top.reshape(subtrees + half_top, rank_dim, rank_dim)
    level_one = jnp.einsum(
        "icab,icvb->iva",
        top_mats[:subtrees].reshape(half_top, 2, rank_dim, rank_dim),
        stacked.reshape(half_top, 2, vec_rows, rank_dim),
        preferred_element_type=jnp.float32,
    ).astype(jnp.bfloat16)
    level_two = jnp.einsum(
        "icab,icvb->iva",
        top_mats[subtrees:].reshape(quarter_top, 2, rank_dim, rank_dim),
        level_one.reshape(quarter_top, 2, vec_rows, rank_dim),
        preferred_element_type=jnp.float32,
    ).astype(jnp.bfloat16)
    top_coef = jnp.concatenate([level_one, level_two], axis=0)
    level_shift = jnp.where(
        jnp.arange(half_top + quarter_top, dtype=jnp.int32)[:, None] >= half_top, half_top, 0
    ).astype(jnp.int32)
    top_out = couple(
        top_coupling.reshape(half_top + quarter_top, top_count, rank_dim, rank_dim),
        top_coef[top_partners + level_shift],
    )
    upper_bar = top_out[half_top:].astype(jnp.bfloat16)
    middle_top = top_out[:half_top] + jnp.einsum(
        "icab,iva->icvb",
        top_mats[subtrees:].reshape(quarter_top, 2, rank_dim, rank_dim),
        upper_bar,
        preferred_element_type=jnp.float32,
    ).reshape(half_top, vec_rows, rank_dim)
    middle_bar = middle_top.astype(jnp.bfloat16)
    mat_mine = lax.dynamic_index_in_dim(top_mats, my_index, 0, keepdims=False)
    parent_mine = lax.dynamic_index_in_dim(middle_bar, my_index // 2, 0, keepdims=False)
    root_down = jnp.einsum("ab,va->vb", mat_mine, parent_mine, preferred_element_type=jnp.float32)
    current = (local_out[node_count - 1] + root_down)[None]
    offset = node_count - 1
    level_count = 1
    for level_idx in range(levels - 1):
        child_count = level_count * 2
        offset = offset - child_count
        pair_mats = transfers[offset : offset + child_count].reshape(
            level_count, 2, rank_dim, rank_dim
        )
        downward = jnp.einsum(
            "icab,iva->icvb",
            pair_mats,
            current.astype(jnp.bfloat16),
            preferred_element_type=jnp.float32,
        ).reshape(child_count, vec_rows, rank_dim)
        current = local_out[offset : offset + child_count] + downward
        level_count = child_count
    far_field = jnp.einsum(
        "tva,tal->tvl", current.astype(jnp.bfloat16), leaf_basis, preferred_element_type=jnp.float32
    )
    answer = (far_field + near_part.reshape(far_field.shape)).astype(jnp.bfloat16)
    return hand_back(
        lines, leaves, answer.reshape(leaves * vec_rows, leaf_pts), point_order.reshape(1, dev_pts)
    )


def solution(mesh):
    in_specs = (
        P(("grp", "vec"), ("leaf", "sub")),
        P("grp", ("leaf", "sub")),
        P(("grp", "leaf", "sub")),
        P(("grp", "leaf", "sub"), None, None),
        P(("grp", "leaf", "sub"), None),
        P("grp", None),
        P(("grp", "leaf", "sub"), None),
        P(("grp", "leaf", "sub"), None, None),
        P("grp", None),
        P("grp", None, None),
    )
    out_specs = P(("grp", "vec"), ("leaf", "sub"))
    return jax.shard_map(
        on_device, mesh=mesh, in_specs=in_specs, out_specs=out_specs, check_vma=False
    )
```

```python
import functools

import jax
import jax.numpy as jnp
from jax import lax
from jax.experimental import pallas as pl
from jax.experimental.pallas import tpu as pltpu
from jax.sharding import PartitionSpec as P

ROOT_THREE = 1.7320508075688772
LENGTH_SCALE = 0.0125
KERNEL_GAIN = 0.25
LOG2_E = 1.4426950408889634
MESH = pl.DeviceIdType.MESH
VMEM_LIMIT = 24 * 1024 * 1024
CHUNK = 1024
FIELDS = 6
AUX_CHUNK = 512


def for_each_block(lines, pairs, sems, process, prepare):
    send_sem, pass_sem, recv_sem = sems
    mine = lax.axis_index("leaf")
    core = lax.axis_index("sub")
    other = 1 - core
    barrier = pltpu.get_barrier_semaphore()

    def greet(target):
        pl.semaphore_signal(barrier, inc=1, device_id=target, device_id_type=MESH)

    def copies(block, target, sem):
        return [
            pltpu.make_async_remote_copy(
                src_ref=held.at[block],
                dst_ref=held.at[block],
                send_sem=sem.at[which, block],
                recv_sem=recv_sem.at[which, block],
                device_id=target,
                device_id_type=MESH,
            )
            for which, (own, held) in enumerate(pairs)
        ]

    def ahead(block, way):
        return copies(block, {"leaf": mine + way}, send_sem.at[(way + 1) // 2])

    def across(block):
        return copies(block, {"sub": other}, pass_sem)

    def has(way):
        return mine > 0 if way < 0 else mine < lines - 1

    def guarded(condition, action):
        pl.when(condition)(action)

    def start(some):
        for copy in some:
            copy.start()

    def wait_sent(some):
        for copy in some:
            copy.wait_send()

    def wait_here(some):
        for copy in some:
            copy.wait_recv()

    greet({"sub": other})
    for way in (-1, 1):
        guarded(has(way), lambda way=way: greet({"leaf": mine + way}))
    for own, held in pairs:
        held[mine * 2 + core] = own[...]
    inside = jnp.logical_and(has(-1), has(1))
    guarded(inside, lambda: pl.semaphore_wait(barrier, 3))
    guarded(jnp.logical_not(inside), lambda: pl.semaphore_wait(barrier, 2))

    me = mine * 2 + core
    for way in (-1, 1):
        guarded(has(way), lambda way=way: start(ahead(me, way)))
    start(across(me))
    prepare()
    process(me)
    wait_here(across(mine * 2 + other))
    process(mine * 2 + other)

    def step(hop, carry):
        for way in (-1, 1):
            line = mine - way * hop
            there = line >= 0 if way > 0 else line < lines
            block = line * 2 + core

            def take(way=way, block=block):
                wait_here(across(block))
                guarded(has(way), lambda: start(ahead(block, way)))
                start(across(block))

            guarded(there, take)
        for way in (-1, 1):
            line = mine - way * hop
            there = line >= 0 if way > 0 else line < lines

            def use(line=line):
                process(line * 2 + core)
                wait_here(across(line * 2 + other))
                process(line * 2 + other)

            guarded(there, use)
        return carry

    lax.fori_loop(1, lines, step, 0)

    def finish(line, carry):
        block = line * 2 + core
        wait_sent(across(block))
        for way in (-1, 1):
            upstream = line <= mine if way > 0 else line >= mine
            guarded(
                jnp.logical_and(upstream, has(way)), lambda way=way: wait_sent(ahead(block, way))
            )
        return carry

    lax.fori_loop(0, lines, finish, 0)


def arrange_kernel(
    lines, leaves, x_ref, aux_ref, v_out, c_out, x_all, aux_all, total, send_sem, pass_sem, recv_sem
):
    me = lax.axis_index("leaf") * 2 + lax.axis_index("sub")
    rows = x_ref.shape[0]
    dev_pts = x_ref.shape[1]
    leaf_pts = v_out.shape[1]
    slots = leaves + 2
    slot_pad = -(-slots // 16) * 16

    def prepare():
        total[...] = jnp.zeros_like(total)

    slot_ids = lax.broadcasted_iota(jnp.int32, (slot_pad, CHUNK), 0).astype(jnp.bfloat16)
    place_ids = lax.broadcasted_iota(jnp.int32, (leaf_pts, CHUNK), 0).astype(jnp.bfloat16)

    def process(block):
        aux = aux_all[block].astype(jnp.float32)
        for part in range(dev_pts // CHUNK):
            at = part * FIELDS * CHUNK // AUX_CHUNK
            fields = jnp.concatenate(
                [aux[at + k : at + k + FIELDS] for k in range(0, FIELDS * CHUNK // AUX_CHUNK, FIELDS)],
                axis=1,
            )
            x = x_all[block, :, part * CHUNK : (part + 1) * CHUNK]
            slot = (fields[5:6] - me.astype(jnp.float32)) * leaves + fields[4:5] + 1.0
            slot = jnp.clip(slot, -1.0, float(slots)).astype(jnp.bfloat16)
            slot_here = jnp.broadcast_to(slot, (rows, CHUNK))
            zero = jnp.zeros_like(x)
            parts = [jnp.where(slot_here == jnp.bfloat16(k), x, zero) for k in range(slots)]
            chosen = slot_ids == jnp.broadcast_to(slot, (slot_pad, CHUNK))
            for axis in range(3):
                row = fields[axis : axis + 1].astype(jnp.bfloat16)
                row = jnp.broadcast_to(row, (slot_pad, CHUNK))
                parts.append(jnp.where(chosen, row, jnp.zeros_like(row)))
            place = jnp.broadcast_to(fields[3:4].astype(jnp.bfloat16), (leaf_pts, CHUNK))
            one_hot = jnp.where(place_ids == place, jnp.bfloat16(1), jnp.bfloat16(0))
            total[...] += lax.dot_general(
                jnp.concatenate(parts, axis=0),
                one_hot,
                (((1,), (1,)), ((), ())),
                preferred_element_type=jnp.float32,
            ).astype(jnp.bfloat16)

    pairs = ((x_ref, x_all), (aux_ref, aux_all))
    for_each_block(lines, pairs, (send_sem, pass_sem, recv_sem), process, prepare)
    v_out[...] = total[: slots * rows, :]
    found = total[slots * rows :, :].astype(jnp.float32)
    c_out[...] = jnp.zeros_like(c_out)
    for slot in range(slots):
        for axis in range(3):
            at = axis * slot_pad + slot
            c_out[slot * 8 + axis : slot * 8 + axis + 1, :] = found[at : at + 1, :]


def arrange(lines, leaves, leaf_pts, x, aux):
    rows, dev_pts = x.shape
    devices = lines * 2
    slots = leaves + 2
    slot_pad = -(-slots // 16) * 16
    return pl.pallas_call(
        functools.partial(arrange_kernel, lines, leaves),
        out_shape=(
            jax.ShapeDtypeStruct((slots * rows, leaf_pts), jnp.bfloat16),
            jax.ShapeDtypeStruct((slots * 8, leaf_pts), jnp.float32),
        ),
        in_specs=[pl.BlockSpec(memory_space=pltpu.VMEM)] * 2,
        out_specs=(pl.BlockSpec(memory_space=pltpu.VMEM),) * 2,
        scratch_shapes=[
            pltpu.VMEM((devices,) + x.shape, jnp.bfloat16),
            pltpu.VMEM((devices,) + aux.shape, jnp.bfloat16),
            pltpu.VMEM((slots * rows + 3 * slot_pad, leaf_pts), jnp.bfloat16),
            pltpu.SemaphoreType.DMA((2, 2, devices)),
            pltpu.SemaphoreType.DMA((2, devices)),
            pltpu.SemaphoreType.DMA((2, devices)),
        ],
        compiler_params=pltpu.CompilerParams(
            collective_id=0, has_side_effects=True, vmem_limit_bytes=VMEM_LIMIT
        ),
        name="arrange",
    )(x, aux)


def hand_back_kernel(
    lines, leaves, y_ref, order_ref, out_ref, y_all, one_hot, leaf_at, send_sem, pass_sem, recv_sem
):
    leaf_pts = y_ref.shape[1]
    rows = y_ref.shape[0] // leaves
    dev_pts = order_ref.shape[1]

    def prepare():
        place_ids = lax.broadcasted_iota(jnp.int32, (leaf_pts, CHUNK), 0).astype(jnp.bfloat16)
        for part in range(dev_pts // CHUNK):
            at = slice(part * CHUNK, (part + 1) * CHUNK)
            order = order_ref[:, at]
            leaf_at[:, at] = (order // leaf_pts).astype(jnp.float32)
            place = (order % leaf_pts).astype(jnp.float32).astype(jnp.bfloat16)
            place = jnp.broadcast_to(place, (leaf_pts, CHUNK))
            one_hot[:, at] = jnp.where(place_ids == place, jnp.bfloat16(1), jnp.bfloat16(0))
        out_ref[...] = jnp.zeros_like(out_ref)

    def process(block):
        y = y_all[block]

        def chunk(part, carry):
            at = pl.ds(pl.multiple_of(part * CHUNK, CHUNK), CHUNK)
            found = jnp.dot(y, one_hot[:, at], preferred_element_type=jnp.float32)
            leaf = leaf_at[:, at] - (block * leaves).astype(jnp.float32)
            leaf = jnp.clip(leaf, -1.0, float(leaves)).astype(jnp.bfloat16)
            leaf = jnp.broadcast_to(leaf, (rows, CHUNK))
            got = jnp.zeros((rows, CHUNK), jnp.bfloat16)
            for k in range(leaves):
                here = found[k * rows : (k + 1) * rows].astype(jnp.bfloat16)
                got = jnp.where(leaf == jnp.bfloat16(k), here, got)
            out_ref[:, at] += got
            return carry

        lax.fori_loop(0, dev_pts // CHUNK, chunk, 0)

    sems = (send_sem, pass_sem, recv_sem)
    for_each_block(lines, ((y_ref, y_all),), sems, process, prepare)


def hand_back(lines, leaves, y, order):
    devices = lines * 2
    rows = y.shape[0] // leaves
    dev_pts = order.shape[1]
    return pl.pallas_call(
        functools.partial(hand_back_kernel, lines, leaves),
        out_shape=jax.ShapeDtypeStruct((rows, dev_pts), jnp.bfloat16),
        in_specs=[pl.BlockSpec(memory_space=pltpu.VMEM)] * 2,
        out_specs=pl.BlockSpec(memory_space=pltpu.VMEM),
        scratch_shapes=[
            pltpu.VMEM((devices,) + y.shape, jnp.bfloat16),
            pltpu.VMEM((y.shape[1], dev_pts), jnp.bfloat16),
            pltpu.VMEM((1, dev_pts), jnp.float32),
            pltpu.SemaphoreType.DMA((2, 1, devices)),
            pltpu.SemaphoreType.DMA((1, devices)),
            pltpu.SemaphoreType.DMA((1, devices)),
        ],
        compiler_params=pltpu.CompilerParams(
            collective_id=1, has_side_effects=True, vmem_limit_bytes=VMEM_LIMIT
        ),
        name="hand_back",
    )(y, order)


def matern(columns, rows):
    squared = None
    for axis in range(3):
        delta = columns[:, axis : axis + 1] - rows[axis : axis + 1, :]
        squared = delta * delta if squared is None else squared + delta * delta
    distance = squared * lax.rsqrt(jnp.maximum(squared, 1e-30))
    rate = ROOT_THREE / LENGTH_SCALE
    rising = KERNEL_GAIN + (KERNEL_GAIN * rate) * distance
    return (rising * jnp.exp2(distance * (-rate * LOG2_E))).astype(jnp.bfloat16)


def near_sums(leaves, v_ref, c_ref, near):
    rows = v_ref.shape[0] // (leaves + 2)
    near[...] = jnp.zeros_like(near)

    def vec_at(slot):
        return pl.ds(pl.multiple_of(slot * rows, rows), rows)

    def coord_at(slot):
        return pl.ds(pl.multiple_of(slot * 8, 8), 8)

    def step(slot, carry):
        here = c_ref[coord_at(slot), :]
        columns = jnp.transpose(here)
        beside = matern(columns, c_ref[coord_at(slot + 1), :])
        within = matern(columns, here)
        x_here = v_ref[vec_at(slot), :]
        x_next = v_ref[vec_at(slot + 1), :]
        near[vec_at(slot + 1), :] += jnp.dot(x_here, beside, preferred_element_type=jnp.float32)
        near[vec_at(slot), :] += jnp.dot(
            x_here, within, preferred_element_type=jnp.float32
        ) + lax.dot_general(
            x_next, beside, (((1,), (1,)), ((), ())), preferred_element_type=jnp.float32
        )
        return carry

    lax.fori_loop(0, leaves + 1, step, 0)


def near_kernel(
    lines,
    leaves,
    v_ref,
    c_ref,
    coef_ref,
    root_ref,
    near_out,
    levels_out,
    roots_out,
    near,
    send_sem,
    recv_sem,
    root_send,
    root_recv,
):
    devices = lines * 2
    nodes = coef_ref.shape[0]
    rows = v_ref.shape[0] // (leaves + 2)
    me = lax.axis_index("leaf") * 2 + lax.axis_index("sub")

    def place(device):
        return {"leaf": device // 2, "sub": lax.rem(device, 2)}

    after = lax.rem(me + 1, devices)
    before = lax.rem(me + devices - 1, devices)
    barrier = pltpu.get_barrier_semaphore()

    def greet(hop, carry):
        pl.semaphore_signal(
            barrier, inc=1, device_id=place(lax.rem(me + hop, devices)), device_id_type=MESH
        )
        return carry

    lax.fori_loop(1, devices, greet, 0)
    pl.semaphore_wait(barrier, devices - 1)

    def root_copy(hop):
        return pltpu.make_async_remote_copy(
            src_ref=root_ref,
            dst_ref=roots_out.at[me],
            send_sem=root_send.at[hop],
            recv_sem=root_recv.at[me],
            device_id=place(lax.rem(me + hop, devices)),
            device_id_type=MESH,
        )

    def start_root(hop, carry):
        root_copy(hop).start()
        return carry

    copies = [
        pltpu.make_async_remote_copy(
            src_ref=coef_ref,
            dst_ref=levels_out.at[which],
            send_sem=send_sem.at[which],
            recv_sem=recv_sem.at[which],
            device_id=place(target),
            device_id_type=MESH,
        )
        for which, target in ((0, after), (2, before))
    ]
    lax.fori_loop(1, devices, start_root, 0)
    for copy in copies:
        copy.start()
    levels_out[1] = coef_ref[...]
    roots_out[me] = root_ref[...]
    near_sums(leaves, v_ref, c_ref, near)
    near_out[...] = near[rows : (leaves + 1) * rows, :]

    def end_root(hop, carry):
        source = lax.rem(me + hop, devices)
        pltpu.make_async_remote_copy(
            src_ref=root_ref,
            dst_ref=roots_out.at[source],
            send_sem=root_send.at[hop],
            recv_sem=root_recv.at[source],
            device_id=place(source),
            device_id_type=MESH,
        ).wait()
        return carry

    lax.fori_loop(1, devices, end_root, 0)
    for copy in copies:
        copy.wait()


def near_and_levels(lines, leaves, v, c, coef, root):
    devices = lines * 2
    rows = v.shape[0] // (leaves + 2)
    return pl.pallas_call(
        functools.partial(near_kernel, lines, leaves),
        out_shape=(
            jax.ShapeDtypeStruct((leaves * rows, v.shape[1]), jnp.float32),
            jax.ShapeDtypeStruct((3,) + coef.shape, jnp.bfloat16),
            jax.ShapeDtypeStruct((devices,) + root.shape, jnp.bfloat16),
        ),
        in_specs=[pl.BlockSpec(memory_space=pltpu.VMEM)] * 4,
        out_specs=(pl.BlockSpec(memory_space=pltpu.VMEM),) * 3,
        scratch_shapes=[
            pltpu.VMEM(v.shape, jnp.float32),
            pltpu.SemaphoreType.DMA((3,)),
            pltpu.SemaphoreType.DMA((3,)),
            pltpu.SemaphoreType.DMA((devices,)),
            pltpu.SemaphoreType.DMA((devices,)),
        ],
        compiler_params=pltpu.CompilerParams(
            collective_id=2, has_side_effects=True, vmem_limit_bytes=VMEM_LIMIT
        ),
        name="near",
    )(v, c, coef, root)


def couple(couplings, gathered_rows):
    return jnp.einsum(
        "gkab,gkvb->gva", couplings, gathered_rows, preferred_element_type=jnp.float32
    )


def on_device(
    vectors,
    coords,
    point_order,
    leaf_basis,
    transfer_local,
    transfer_top,
    partners_local,
    coupling_local,
    top_partners,
    top_coupling,
):
    vec_rows = vectors.shape[0]
    dev_pts = vectors.shape[1]
    subtrees = lax.axis_size(("leaf", "sub"))
    leaves = leaf_basis.shape[0]
    rank_dim = leaf_basis.shape[1]
    leaf_pts = leaf_basis.shape[2]
    node_count = 2 * leaves - 1
    levels = leaves.bit_length()
    partners = partners_local.shape[1]
    top_count = top_partners.shape[1]
    my_index = lax.axis_index(("leaf", "sub"))
    lines = lax.axis_size("leaf")
    fields = jnp.concatenate(
        [
            coords,
            (point_order % leaf_pts)[None].astype(jnp.bfloat16),
            (point_order // leaf_pts % leaves)[None].astype(jnp.bfloat16),
            (point_order // dev_pts)[None].astype(jnp.bfloat16),
        ],
        axis=0,
    )
    aux = fields.reshape(FIELDS, dev_pts // AUX_CHUNK, AUX_CHUNK).transpose(1, 0, 2)
    aux = aux.reshape(FIELDS * dev_pts // AUX_CHUNK, AUX_CHUNK)
    v_slots, c_slots = arrange(lines, leaves, leaf_pts, vectors, aux)
    leaf_rows = v_slots.reshape(leaves + 2, vec_rows, leaf_pts)[1 : leaves + 1]
    coefficients = jnp.einsum(
        "tvl,tal->tva", leaf_rows, leaf_basis, preferred_element_type=jnp.float32
    ).astype(jnp.bfloat16)
    transfers = transfer_local.reshape(2 * leaves - 2, rank_dim, rank_dim)
    couplings = coupling_local.reshape(node_count, partners, rank_dim, rank_dim)
    per_level = [coefficients]
    offset = 0
    level_count = leaves
    for level_idx in range(levels - 1):
        pair_mats = transfers[offset : offset + level_count].reshape(
            level_count // 2, 2, rank_dim, rank_dim
        )
        pair_coef = per_level[-1].reshape(level_count // 2, 2, vec_rows, rank_dim)
        per_level.append(
            jnp.einsum(
                "icab,icvb->iva", pair_mats, pair_coef, preferred_element_type=jnp.float32
            ).astype(jnp.bfloat16)
        )
        offset = offset + level_count
        level_count = level_count // 2
    all_levels = jnp.concatenate(per_level, axis=0)
    near_part, padded_all, stacked = near_and_levels(
        lines,
        leaves,
        v_slots,
        c_slots,
        all_levels.reshape(node_count * vec_rows, rank_dim),
        per_level[-1].reshape(vec_rows, rank_dim),
    )
    padded_all = padded_all.reshape(3 * node_count, vec_rows, rank_dim)
    local_idx = partners_local - (my_index - 1) * node_count
    local_out = couple(couplings, padded_all[local_idx])
    half_top = subtrees // 2
    quarter_top = subtrees // 4
    top_mats = transfer_top.reshape(subtrees + half_top, rank_dim, rank_dim)
    level_one = jnp.einsum(
        "icab,icvb->iva",
        top_mats[:subtrees].reshape(half_top, 2, rank_dim, rank_dim),
        stacked.reshape(half_top, 2, vec_rows, rank_dim),
        preferred_element_type=jnp.float32,
    ).astype(jnp.bfloat16)
    level_two = jnp.einsum(
        "icab,icvb->iva",
        top_mats[subtrees:].reshape(quarter_top, 2, rank_dim, rank_dim),
        level_one.reshape(quarter_top, 2, vec_rows, rank_dim),
        preferred_element_type=jnp.float32,
    ).astype(jnp.bfloat16)
    top_coef = jnp.concatenate([level_one, level_two], axis=0)
    level_shift = jnp.where(
        jnp.arange(half_top + quarter_top, dtype=jnp.int32)[:, None] >= half_top, half_top, 0
    ).astype(jnp.int32)
    top_out = couple(
        top_coupling.reshape(half_top + quarter_top, top_count, rank_dim, rank_dim),
        top_coef[top_partners + level_shift],
    )
    upper_bar = top_out[half_top:].astype(jnp.bfloat16)
    middle_top = top_out[:half_top] + jnp.einsum(
        "icab,iva->icvb",
        top_mats[subtrees:].reshape(quarter_top, 2, rank_dim, rank_dim),
        upper_bar,
        preferred_element_type=jnp.float32,
    ).reshape(half_top, vec_rows, rank_dim)
    middle_bar = middle_top.astype(jnp.bfloat16)
    mat_mine = lax.dynamic_index_in_dim(top_mats, my_index, 0, keepdims=False)
    parent_mine = lax.dynamic_index_in_dim(middle_bar, my_index // 2, 0, keepdims=False)
    root_down = jnp.einsum("ab,va->vb", mat_mine, parent_mine, preferred_element_type=jnp.float32)
    current = (local_out[node_count - 1] + root_down)[None]
    offset = node_count - 1
    level_count = 1
    for level_idx in range(levels - 1):
        child_count = level_count * 2
        offset = offset - child_count
        pair_mats = transfers[offset : offset + child_count].reshape(
            level_count, 2, rank_dim, rank_dim
        )
        downward = jnp.einsum(
            "icab,iva->icvb",
            pair_mats,
            current.astype(jnp.bfloat16),
            preferred_element_type=jnp.float32,
        ).reshape(child_count, vec_rows, rank_dim)
        current = local_out[offset : offset + child_count] + downward
        level_count = child_count
    far_field = jnp.einsum(
        "tva,tal->tvl", current.astype(jnp.bfloat16), leaf_basis, preferred_element_type=jnp.float32
    )
    answer = (far_field + near_part.reshape(far_field.shape)).astype(jnp.bfloat16)
    return hand_back(
        lines, leaves, answer.reshape(leaves * vec_rows, leaf_pts), point_order.reshape(1, dev_pts)
    )


def solution(mesh):
    in_specs = (
        P(("grp", "vec"), ("leaf", "sub")),
        P("grp", ("leaf", "sub")),
        P(("grp", "leaf", "sub")),
        P(("grp", "leaf", "sub"), None, None),
        P(("grp", "leaf", "sub"), None),
        P("grp", None),
        P(("grp", "leaf", "sub"), None),
        P(("grp", "leaf", "sub"), None, None),
        P("grp", None),
        P("grp", None, None),
    )
    out_specs = P(("grp", "vec"), ("leaf", "sub"))
    return jax.shard_map(
        on_device, mesh=mesh, in_specs=in_specs, out_specs=out_specs, check_vma=False
    )
```
